32 devices in a mesh: segment: 4 (over y, core), ctx: 4 (over z), tp: 2 (over x).
Axes of the slice: x: 2, y: 2, z: 4, core: 2. Of those that a mesh axis runs over, the one named last changes fastest.
Arguments:
- held: bfloat16 [4, 1024, 3584], P('segment', 'ctx'), may hold values from -6 to 6
- text: bfloat16 [1024, 3584], P('ctx'), may hold values from -6 to 6
- frames: bfloat16 [512, 1024], P('ctx'), may hold values from -6 to 6
- join: int32 [8], P('ctx'), may hold values from 0 to 960, as said below
- ln_gain: float32 [1024], replicated, may hold values from 0.1 to 1.9
- w_proj: bfloat16 [1024, 3584], P('tp'), may hold values from -0.1875 to 0.1875
- b_proj: float32 [3584], replicated, may hold values from -3 to 3
- norm_gain: float32 [3, 3584], replicated, may hold values from 0.1 to 1.9
- w_qkv: bfloat16 [3, 3584, 2304], P(None, 'ctx', 'tp'), may hold values from -0.09375 to 0.09375
- b_qkv: float32 [3, 2304], P(None, 'tp'), may hold values from -4 to 4
- w_out: bfloat16 [3, 1792, 3584], P(None, 'tp', 'ctx'), may hold values from -1.5 to 1.5
Outputs:
- segment_out: bfloat16 [4, 1024, 3584], P('segment', 'ctx')
The draws below stay inside these ranges and needn't reach their ends.
Inputs may be any that keep to these rules, and one draw needn't show every extreme that they name: `join`: frames never intersect; the 2 frames f with f // 2 == d lie in order inside positions d * 256 to (d + 1) * 256 - 1.
All inputs are finite; a program needn't handle non-finite values.
Results may differ from the reference program's by a relative error of at most 0.015.
Values may be sent and summed in bfloat16 or wider, within the bound.
A program may use at most 128 MiB of HBM per device.

```python
import math
import jax
import jax.numpy as jnp
from jax import lax

D = 3584
HD = 128
KVH = 2
GROUP = 7
VD = 1024
FRAME = 64
FR_DEV = 2
TOK_DEV = 256
QH = 14
QKV = 2304
LAYERS = 3
TOKENS = 1024
FRAMES = 8
VIS = 512
N_SEGMENT = 4


def draw_join(key, part):
    devices = FRAMES // FR_DEV
    spare = TOK_DEV - FR_DEV * FRAME
    cuts = jax.random.randint(key, (devices, FR_DEV), 0, spare + 1).astype(jnp.int32)
    cuts = jnp.sort(cuts, axis=1)
    device_ids = jnp.arange(devices, dtype=jnp.int32)[:, None]
    cuts = jnp.where(device_ids == 0, 0, jnp.where(device_ids == devices - 1, spare, cuts))
    starts = device_ids * TOK_DEV + cuts + jnp.arange(FR_DEV, dtype=jnp.int32)[None, :] * FRAME
    return starts.reshape(-1).astype(jnp.int32)


def draw_b_qkv(key, part):
    base = jnp.clip(0.5 * jax.random.normal(key, (LAYERS, KVH, GROUP + 2, HD), jnp.float32), -3.0, 3.0)
    return base.reshape(LAYERS, QKV).astype(jnp.float32)


def levels(key, shape, cuts, least, high):
    loudness = 1.0
    for dim, parts in cuts:
        steps = jax.random.uniform(jax.random.fold_in(jax.random.fold_in(key, 6), dim), (parts,), jnp.float32, least / len(cuts), high / len(cuts))
        loudness = loudness * jnp.repeat(jnp.exp(steps), shape[dim] // parts).reshape((-1,) + (1,) * (len(shape) - 1 - dim))
    return loudness


def noise(key, extent, scale, most, cuts=(), kind=jnp.bfloat16):
    entries = scale * jax.random.normal(key, extent, jnp.float32)
    if cuts:
        entries = entries * levels(key, extent, cuts, -0.22, 0.18)
    return jnp.clip(entries, -most, most).astype(kind)


def setup_inputs(seed: int = 0) -> dict:
    seeds = jax.random.split(jax.random.key(seed), 12)
    held = noise(seeds[0], (N_SEGMENT, TOKENS, D), 1.0, 6.0, ((0, 4), (1, 4)))
    text = noise(seeds[1], (TOKENS, D), 1.0, 6.0, ((0, 4),))
    frames = noise(seeds[2], (VIS, VD), 1.0, 6.0, ((0, 4),))
    join = draw_join(jax.random.fold_in(seeds[11], 71), 0)
    ln_gain = jnp.clip(1.0 + 0.18 * jax.random.normal(seeds[4], (VD,), jnp.float32), 0.1, 1.9)
    w_proj = noise(seeds[5], (VD, D), VD ** -0.5, 0.1875, ((0, 2),))
    b_proj = noise(seeds[6], (D,), 0.5, 3.0, (), jnp.float32)
    norm_gain = jnp.clip(1.0 + 0.18 * jax.random.normal(seeds[7], (LAYERS, D), jnp.float32), 0.1, 1.9)
    w_qkv = noise(seeds[8], (LAYERS, D, QKV), D ** -0.5, 0.09375, ((1, 4), (2, 2)))
    b_qkv = draw_b_qkv(jax.random.fold_in(seeds[11], 71), 0)
    w_out = noise(seeds[10], (LAYERS, QH * HD, D), 0.25, 1.5, ((1, 2), (2, 4)))
    return {"held": held, "text": text, "frames": frames, "join": join, "ln_gain": ln_gain, "w_proj": w_proj, "b_proj": b_proj, "norm_gain": norm_gain, "w_qkv": w_qkv, "b_qkv": b_qkv, "w_out": w_out}


def vision_rows(text, frames, join, ln_gain, w_proj, b_proj):
    inputs = frames.astype(jnp.float32)
    center = lax.optimization_barrier(jnp.mean(inputs, axis=1, keepdims=True))
    spread = lax.optimization_barrier(jnp.mean((inputs - center) * (inputs - center), axis=1, keepdims=True))
    normed_in = ((inputs - center) * lax.rsqrt(spread + 1e-06) * ln_gain.astype(jnp.float32)).astype(jnp.bfloat16)
    projected = jnp.dot(normed_in, w_proj, preferred_element_type=jnp.float32) + b_proj.astype(jnp.float32)
    positions = jnp.arange(TOKENS, dtype=jnp.int32)[:, None]
    starts = join.astype(jnp.int32)[None, :]
    inside = (positions >= starts) & (positions < starts + FRAME)
    frame_base = (jnp.arange(FRAMES, dtype=jnp.int32) * FRAME)[None, :]
    source = lax.optimization_barrier(jnp.sum(jnp.where(inside, frame_base + positions - starts, 0), axis=1)).astype(jnp.int32)
    is_vision = jnp.any(inside, axis=1)
    taken = jnp.take(projected, source, axis=0)
    return jnp.where(is_vision[:, None], taken, text.astype(jnp.float32)).astype(jnp.bfloat16)

def attention_layer(hidden_in, gain, weight_qkv, bias_qkv, weight_out):
    inputs = hidden_in.astype(jnp.float32)
    normed = (inputs * lax.rsqrt(lax.optimization_barrier(jnp.mean(inputs * inputs, axis=1, keepdims=True)) + 1e-06) * gain.astype(jnp.float32)).astype(jnp.bfloat16)
    merged = (jnp.dot(normed, weight_qkv, preferred_element_type=jnp.float32) + bias_qkv.astype(jnp.float32)).astype(jnp.bfloat16)
    grouped = merged.reshape(TOKENS, KVH, GROUP + 2, HD)
    queries = grouped[:, :, :GROUP, :]
    keys = grouped[:, :, GROUP, :].astype(jnp.float32)
    values = grouped[:, :, GROUP + 1, :].astype(jnp.float32)
    block_len = math.gcd(TOKENS, 512)
    block_count = TOKENS // block_len
    query_blocks = queries.reshape(block_count, block_len, KVH, GROUP, HD)
    key_pos = jnp.arange(TOKENS, dtype=jnp.int32)

    def one_block(packed):
        block_index, block_query = packed
        query_pos = block_index.astype(jnp.int32) * block_len + jnp.arange(block_len, dtype=jnp.int32)
        scores = jnp.einsum('qkgd,tkd->kgqt', block_query.astype(jnp.float32), keys) * HD ** (-0.5)
        allowed = (key_pos[None, :] <= query_pos[:, None])[None, None]
        scores = jnp.where(allowed, scores, -1e+30)
        peak = lax.optimization_barrier(jnp.max(scores, axis=-1, keepdims=True))
        weights = jnp.where(allowed, jnp.exp(scores - peak), 0.0)
        total = lax.optimization_barrier(jnp.sum(weights, axis=-1))
        rounded = lax.optimization_barrier(weights.astype(jnp.bfloat16)).astype(jnp.float32)
        mixed = jnp.einsum('kgqt,tkd->qkgd', rounded, values) / jnp.transpose(total, (2, 0, 1))[..., None]
        return mixed.astype(jnp.bfloat16).reshape(block_len, KVH * GROUP * HD)
    attended = lax.map(one_block, (jnp.arange(block_count, dtype=jnp.int32), query_blocks))
    attended = attended.reshape(TOKENS, QH * HD)
    return (inputs + jnp.dot(attended, weight_out, preferred_element_type=jnp.float32)).astype(jnp.bfloat16)

def reference(held, text, frames, join, ln_gain, w_proj, b_proj, norm_gain, w_qkv, b_qkv, w_out):
    results = [vision_rows(text, frames, join, ln_gain, w_proj, b_proj)]
    for layer_id in range(LAYERS):
        results.append(attention_layer(held[layer_id], norm_gain[layer_id], w_qkv[layer_id], b_qkv[layer_id], w_out[layer_id]))
    return jnp.stack(results)
```

```python
from functools import partial

import jax
import jax.numpy as jnp
from jax import lax
from jax.experimental import pallas as pl
from jax.experimental.pallas import tpu as pltpu
from jax.sharding import PartitionSpec as P

HD = 128
GROUP = 7
FRAME = 64


def shifted(value, axis, by):
    devices = lax.axis_size(axis)
    pairs = [(i, i + by) for i in range(devices) if 0 <= i + by < devices]
    return lax.ppermute(value, axis, pairs)


def update_state(softmax_state, query_flat, query_pos, keys_in, values_in, offset):
    peak_old, total_old, accum_old = softmax_state
    key_pos = jnp.arange(keys_in.shape[0], dtype=jnp.int32)
    scores = jnp.dot(query_flat, keys_in.T, preferred_element_type=jnp.float32) * HD ** (-0.5)
    allowed = key_pos[None, :] <= query_pos[:, None]
    scores = jnp.where(allowed, scores, -1e30)
    peak_new = jnp.maximum(peak_old, jnp.max(scores, axis=1))
    weights = jnp.where(allowed, jnp.exp(scores - peak_new[:, None]), 0.0)
    total_new = jnp.sum(weights, axis=1)
    accum_new = jnp.dot(weights.astype(jnp.bfloat16), values_in, preferred_element_type=jnp.float32)
    return (peak_new, total_new, accum_new)


def keep_state(softmax_state):
    return softmax_state


def on_device(held, text, frames, join, ln_gain, w_proj, b_proj, norm_gain, w_qkv, b_qkv, w_out):
    segment_id = lax.axis_index("segment")
    ctx_id = lax.axis_index("ctx")
    tp_id = lax.axis_index("tp")
    hidden_in = shifted(held[0], "segment", 1)
    tok_rows = hidden_in.shape[0]
    half_rows = tok_rows // 2
    layer_id = jnp.maximum(segment_id - 1, 0)
    weight_qkv = lax.dynamic_index_in_dim(w_qkv, layer_id, 0, keepdims=False)
    bias_qkv = lax.dynamic_index_in_dim(b_qkv, layer_id, 0, keepdims=False)
    layer_gain = lax.dynamic_index_in_dim(norm_gain, layer_id, 0, keepdims=False)
    weight_out = lax.dynamic_index_in_dim(w_out, layer_id, 0, keepdims=False)
    inputs = hidden_in.astype(jnp.float32)
    normed = (
        inputs * lax.rsqrt(jnp.mean(inputs * inputs, axis=1, keepdims=True) + 1e-06) * layer_gain
    ).astype(jnp.bfloat16)
    merged = jnp.dot(
        normed,
        lax.all_gather(weight_qkv, "ctx", axis=0, tiled=True),
        preferred_element_type=jnp.float32,
    )
    merged = (merged + bias_qkv).astype(jnp.bfloat16)
    query_cols = GROUP * HD
    queries = merged[:, :query_cols]
    key_part = merged[:, query_cols : query_cols + HD]
    value_part = merged[:, query_cols + HD : query_cols + 2 * HD]
    local_steps = jnp.arange(half_rows, dtype=jnp.int32)
    first_pos = ctx_id * tok_rows + local_steps
    second_q = queries[half_rows:]
    second_pos = ctx_id * tok_rows + half_rows + local_steps
    first_flat = queries[:half_rows].reshape(half_rows * GROUP, HD)
    second_flat = second_q.reshape(half_rows * GROUP, HD)
    first_qpos = jnp.repeat(first_pos, GROUP)
    second_qpos = jnp.repeat(second_pos, GROUP)
    flat_rows = half_rows * GROUP
    empty = (
        jnp.full((flat_rows,), -1e30, jnp.float32),
        jnp.zeros((flat_rows,), jnp.float32),
        jnp.zeros((flat_rows, HD), jnp.float32),
    )
    carried = (empty, empty)
    offset = jnp.int32(0)
    keys_in = lax.all_gather(key_part, "ctx", axis=0, tiled=True)
    values_in = lax.all_gather(value_part, "ctx", axis=0, tiled=True)
    updated = []
    for softmax_state, query_flat, query_pos in (
        (carried[0], first_flat, first_qpos),
        (carried[1], second_flat, second_qpos),
    ):
        step_fn = partial(
            update_state,
            query_flat=query_flat,
            query_pos=query_pos,
            keys_in=keys_in,
            values_in=values_in,
            offset=offset,
        )
        updated.append(lax.cond(offset <= jnp.max(query_pos), step_fn, keep_state, softmax_state))

    def finish(softmax_state):
        return (
            (softmax_state[2] / softmax_state[1][:, None])
            .astype(jnp.bfloat16)
            .reshape(half_rows, GROUP * HD)
        )

    first_out = finish(updated[0])
    second_out = finish(updated[1])
    attended = jnp.concatenate([first_out, second_out], axis=0)
    partial_model = jnp.dot(
        attended,
        lax.all_gather(weight_out, "ctx", axis=1, tiled=True),
        preferred_element_type=jnp.float32,
    )
    positions = ctx_id * tok_rows + jnp.arange(tok_rows, dtype=jnp.int32)[:, None]
    starts = join[None, :]
    inside = (positions >= starts) & (positions < starts + FRAME)
    frame_base = (jnp.arange(join.shape[0], dtype=jnp.int32) * FRAME)[None, :]
    source = jnp.sum(jnp.where(inside, frame_base + positions - starts, 0), axis=1)
    is_vision = jnp.any(inside, axis=1)

    def vision_term():
        frame_in = frames.astype(jnp.float32)
        center = jnp.mean(frame_in, axis=1, keepdims=True)
        spread = jnp.mean((frame_in - center) * (frame_in - center), axis=1, keepdims=True)
        normed_frames = ((frame_in - center) * lax.rsqrt(spread + 1e-06) * ln_gain).astype(
            jnp.bfloat16
        )
        vis_width = w_proj.shape[0]
        normed_half = lax.dynamic_slice_in_dim(normed_frames, tp_id * vis_width, vis_width, 1)
        projected = jnp.dot(normed_half, w_proj, preferred_element_type=jnp.float32)
        return jnp.where(is_vision[:, None], jnp.take(projected, source, axis=0), 0.0)

    def model_term():
        return partial_model

    is_first = segment_id == 0
    section_term = lax.cond(is_first, vision_term, model_term)
    baseline = jnp.where(
        is_first, jnp.where(is_vision[:, None], b_proj[None, :], text.astype(jnp.float32)), inputs
    )
    summed = lax.psum(section_term.astype(jnp.bfloat16), "tp").astype(jnp.float32)
    result = (baseline + summed).astype(jnp.bfloat16)
    return result[None]


def relay_kernel(
    sizes,
    held, text, frames, join, ln_gain, w_proj, b_proj, norm_gain, w_qkv, b_qkv, w_out,
    out,
    held_v, rs_out, rs_in, x_v, wq_v, wo_v, own_sum, part_out, part_in, merged_v, kv_v, att_v,
    vis_v, wp_v, text_v, half_out, half_in, half_own, res_v,
    load_sem, store_sem, x_send, x_recv, rs_send, rs_recv, fwd_send, fwd_recv,
    part_send, part_recv, kv_send, kv_recv, att_send, att_recv,
    half_send, half_recv, res_send, res_recv, pair_send, pair_recv,
):
    segs, n, rows, width = sizes
    half = rows // 2
    s = lax.axis_index("segment")
    c = lax.axis_index("ctx")
    t = lax.axis_index("tp")
    layer = jnp.maximum(s - 1, 0)
    is_layer = s > 0
    feeds = s < segs - 1
    query_cols = GROUP * HD

    def remote(src, dst, send, recv, segment, ctx, tp):
        return pltpu.make_async_remote_copy(
            src_ref=src, dst_ref=dst, send_sem=send, recv_sem=recv,
            device_id={"segment": segment, "ctx": ctx, "tp": tp},
            device_id_type=pl.DeviceIdType.MESH,
        )

    def cols(k):
        return pl.ds(pl.multiple_of(k * width, 128), width)

    def turn(d):
        return lax.rem(c + d, n)

    loads = {
        "held": pltpu.make_async_copy(held, held_v, load_sem.at[0]),
        "wq": pltpu.make_async_copy(w_qkv.at[layer], wq_v, load_sem.at[1]),
        "wo": pltpu.make_async_copy(w_out.at[layer], wo_v, load_sem.at[2]),
        "wp": pltpu.make_async_copy(w_proj, wp_v, load_sem.at[3]),
        "text": pltpu.make_async_copy(text, text_v, load_sem.at[4]),
    }

    @pl.when(feeds)
    def _():
        loads["held"].start()

    @pl.when(is_layer)
    def _():
        loads["wq"].start()
        loads["wo"].start()

    @pl.when(s == 0)
    def _():
        loads["wp"].start()
        loads["text"].start()

    barrier = pltpu.get_barrier_semaphore()

    def greet(segment, ctx, tp):
        pl.semaphore_signal(
            barrier, inc=1, device_id={"segment": segment, "ctx": ctx, "tp": tp},
            device_id_type=pl.DeviceIdType.MESH,
        )

    greet(s, c, 1 - t)
    for d in range(1, n):
        greet(s, turn(d), t)

    @pl.when(feeds)
    def _():
        for d in range(n):
            greet(s + 1, turn(d), t)

    @pl.when(is_layer)
    def _():
        for d in range(n):
            greet(s - 1, turn(d), t)

    peers = n + n * jnp.minimum(s, 1) + n * jnp.minimum(segs - 1 - s, 1)
    pl.semaphore_wait(barrier, peers)

    def x_copy(k):
        return remote(
            held.at[pl.ds(pl.multiple_of(t * half, 16), half), cols(k)], x_v.at[c, t],
            x_send.at[k], x_recv.at[c], s + 1, k, t,
        )

    def rs_copy():
        return remote(rs_out, rs_in, rs_send.at[0], rs_recv.at[0], s + 1, c, t)

    def fwd_copy(j, side):
        return remote(
            x_v.at[j, side], x_v.at[j, side], fwd_send.at[j], fwd_recv.at[j], s, c, 1 - t
        )

    def part_copy(j, slot):
        return remote(
            part_out.at[j], part_in.at[slot], part_send.at[j], part_recv.at[slot], s, j, t
        )

    def kv_copy(j, slot):
        return remote(kv_v.at[slot], kv_v.at[slot], kv_send.at[j], kv_recv.at[slot], s, j, t)

    def att_copy(j, slot):
        return remote(att_v.at[slot], att_v.at[slot], att_send.at[j], att_recv.at[slot], s, j, t)

    def half_copy(j):
        return remote(
            half_out.at[j], half_in.at[j], half_send.at[j], half_recv.at[j], s, c, 1 - t
        )

    def res_copy(j, slot):
        return remote(
            half_out.at[n + j], res_v.at[slot, t], res_send.at[j], res_recv.at[slot], s, j, t
        )

    def pair_copy(k, side):
        return remote(
            res_v.at[k, side], res_v.at[k, side], pair_send.at[k], pair_recv.at[k], s, c, 1 - t
        )

    def out_copy(k, side):
        return pltpu.make_async_copy(
            res_v.at[k, side],
            out.at[pl.ds(pl.multiple_of(side * half, 16), half), cols(k)],
            store_sem.at[k, side],
        )

    @pl.when(feeds)
    def _():
        for d in range(n):
            x_copy(turn(d)).start()
        loads["held"].wait()

        @pl.loop(0, rows // 32)
        def _(i):
            at = pl.ds(pl.multiple_of(i * 32, 32), 32)
            x = held_v[at, :].astype(jnp.float32)
            scale = lax.rsqrt(jnp.mean(x * x, axis=1, keepdims=True) + 1e-06)
            rs_out[at, :] = jnp.broadcast_to(scale, (32, HD))

        rs_copy().start()

    @pl.when(s == 0)
    def _():
        frame_in = frames[...].astype(jnp.float32)
        center = jnp.mean(frame_in, axis=1, keepdims=True)
        spread = jnp.mean((frame_in - center) * (frame_in - center), axis=1, keepdims=True)
        normed = ((frame_in - center) * lax.rsqrt(spread + 1e-06) * ln_gain[...]).astype(
            jnp.bfloat16
        )
        vis_width = w_proj.shape[0]
        normed = jnp.where(t == 0, normed[:, :vis_width], normed[:, vis_width:])
        count = frames.shape[0]
        token = lax.broadcasted_iota(jnp.int32, (half, count), 1)
        for side in range(2):
            position = c * rows + side * half + lax.broadcasted_iota(jnp.int32, (half, count), 0)
            pick = jnp.zeros((half, count), jnp.float32)
            for f in range(count // FRAME):
                mine = (token >= f * FRAME) & (token < (f + 1) * FRAME)
                hit = mine & (position - join[f] == token - f * FRAME)
                pick = jnp.where(hit, 1.0, pick)
            vis_v[side] = jnp.dot(
                pick.astype(jnp.bfloat16), normed, preferred_element_type=jnp.float32
            ).astype(jnp.bfloat16)
        loads["wp"].wait()
        loads["text"].wait()

        @pl.loop(0, n)
        def _(k):
            half_out[k] = jnp.dot(
                vis_v[1 - t], wp_v[:, cols(k)], preferred_element_type=jnp.float32
            ).astype(jnp.bfloat16)
            half_copy(k).start()
            half_own[k] = jnp.dot(
                vis_v[t], wp_v[:, cols(k)], preferred_element_type=jnp.float32
            )

        place = c * rows + t * half + lax.broadcasted_iota(jnp.int32, (half, width), 0)
        inside = jnp.zeros((half, width), jnp.bool_)
        for f in range(count // FRAME):
            inside = inside | ((place >= join[f]) & (place < join[f] + FRAME))

        @pl.loop(0, n)
        def _(k):
            half_copy(k).wait_recv()
            total = half_own[k] + half_in[k].astype(jnp.float32) + b_proj[:, cols(k)]
            base = text_v[pl.ds(pl.multiple_of(t * half, 16), half), cols(k)].astype(jnp.float32)
            res_v[k, t] = jnp.where(inside, total, base).astype(jnp.bfloat16)
            pair_copy(k, t).start()
            out_copy(k, t).start()

    @pl.when(is_layer)
    def _():
        loads["wq"].wait()
        gain = norm_gain[pl.ds(layer, 1), cols(c)]

        @pl.loop(0, n)
        def _(d):
            j = turn(d)
            x_wait = remote(
                x_v.at[j, t], x_v.at[j, t], x_send.at[j], x_recv.at[j], s, c, 1 - t
            )
            x_wait.wait_recv()
            fwd_copy(j, t).start()

        @pl.loop(0, n)
        def _(d):
            j = turn(d + 1)
            fwd_copy(j, 1 - t).wait_recv()
            x = x_v[j].reshape(rows, width).astype(jnp.float32)
            product = jnp.dot(
                (x * gain).astype(jnp.bfloat16), wq_v[...], preferred_element_type=jnp.float32
            )

            @pl.when(j == c)
            def _():
                own_sum[...] = product

            @pl.when(j != c)
            def _():
                part_out[j] = product.astype(jnp.bfloat16)
                part_copy(j, c).start()

        for d in range(1, n):
            j = turn(d)
            part_copy(j, j).wait_recv()
            own_sum[...] += part_in[j].astype(jnp.float32)
        remote(rs_out, rs_in, rs_send.at[0], rs_recv.at[0], s, c, 1 - t).wait_recv()
        bias = b_qkv[pl.ds(layer, 1), :]
        merged = (own_sum[...] * rs_in[:, :1] + bias).astype(jnp.bfloat16)
        merged_v[...] = merged[:, :query_cols]
        kv_v[c] = merged[:, query_cols:]
        for k in range(n):
            @pl.when(k > c)
            def _():
                kv_copy(k, c).start()
                kv_v[k] = jnp.zeros((rows, 2 * HD), jnp.bfloat16)

        for k in range(n):
            @pl.when(k < c)
            def _():
                kv_copy(k, k).wait_recv()

        query_pos = c * rows + lax.broadcasted_iota(jnp.int32, (rows, n * rows), 0)
        allowed = lax.broadcasted_iota(jnp.int32, (rows, n * rows), 1) <= query_pos
        keys = kv_v[:, :, :HD].reshape(n * rows, HD)
        values = kv_v[:, :, HD:].reshape(n * rows, HD)
        for h in range(GROUP):
            q = merged_v[:, h * HD : (h + 1) * HD]
            scores = lax.dot_general(
                q, keys, (((1,), (1,)), ((), ())), preferred_element_type=jnp.float32
            ) * HD ** (-0.5)
            scores = jnp.where(allowed, scores, -1e30)
            weights = jnp.exp(scores - jnp.max(scores, axis=1, keepdims=True))
            total = jnp.sum(weights, axis=1, keepdims=True)
            mixed = jnp.dot(
                weights.astype(jnp.bfloat16), values, preferred_element_type=jnp.float32
            ) / total
            att_v[c, :, :, h * HD : (h + 1) * HD] = mixed.astype(jnp.bfloat16).reshape(2, half, HD)
        for d in range(1, n):
            att_copy(turn(d), c).start()
        loads["wo"].wait()

        @pl.loop(0, n)
        def _(d):
            j = turn(d)

            @pl.when(d > 0)
            def _():
                att_copy(j, j).wait_recv()

            half_out[j] = jnp.dot(
                att_v[j, 1 - t], wo_v[...], preferred_element_type=jnp.float32
            ).astype(jnp.bfloat16)
            half_copy(j).start()
            half_own[j] = x_v[j, t].astype(jnp.float32) + jnp.dot(
                att_v[j, t], wo_v[...], preferred_element_type=jnp.float32
            )

        @pl.loop(0, n)
        def _(d):
            j = turn(d)
            half_copy(j).wait_recv()
            total = (half_own[j] + half_in[j].astype(jnp.float32)).astype(jnp.bfloat16)

            @pl.when(d == 0)
            def _():
                res_v[c, t] = total
                pair_copy(c, t).start()
                out_copy(c, t).start()

            @pl.when(d > 0)
            def _():
                half_out[n + j] = total
                res_copy(j, c).start()

        @pl.loop(1, n)
        def _(d):
            k = turn(d)
            res_copy(k, k).wait_recv()
            pair_copy(k, t).start()
            out_copy(k, t).start()

    @pl.loop(0, n)
    def _(d):
        k = turn(d)
        pair_copy(k, 1 - t).wait_recv()
        out_copy(k, 1 - t).start()

    @pl.when(feeds)
    def _():
        for k in range(n):
            x_copy(k).wait_send()
        rs_copy().wait_send()

    @pl.when(is_layer)
    def _():
        @pl.loop(0, n)
        def _(d):
            j = turn(d)
            fwd_copy(j, t).wait_send()

            @pl.when(d > 0)
            def _():
                part_copy(j, c).wait_send()
                att_copy(j, c).wait_send()
                res_copy(j, c).wait_send()

            @pl.when(j > c)
            def _():
                kv_copy(j, c).wait_send()

    @pl.loop(0, n)
    def _(k):
        half_copy(k).wait_send()
        pair_copy(k, t).wait_send()
        out_copy(k, 0).wait()
        out_copy(k, 1).wait()


def relayed(sizes, held, text, frames, join, ln_gain, w_proj, b_proj, norm_gain, w_qkv, b_qkv, w_out):
    segs, n, rows, width = sizes
    half = rows // 2
    depth, qkv = w_qkv.shape[1:]
    bf16, f32 = jnp.bfloat16, jnp.float32
    hbm = pl.BlockSpec(memory_space=pl.ANY)
    vmem = pl.BlockSpec(memory_space=pltpu.VMEM)
    smem = pl.BlockSpec(memory_space=pltpu.SMEM)
    dma = pltpu.SemaphoreType.DMA
    out = pl.pallas_call(
        partial(relay_kernel, sizes),
        out_shape=jax.ShapeDtypeStruct((rows, n * width), bf16),
        in_specs=[hbm, hbm, vmem, smem, vmem, hbm, vmem, vmem, hbm, vmem, hbm],
        out_specs=hbm,
        scratch_shapes=[
            pltpu.VMEM((rows, n * width), bf16),
            pltpu.VMEM((rows, HD), f32),
            pltpu.VMEM((rows, HD), f32),
            pltpu.VMEM((n, 2, half, width), bf16),
            pltpu.VMEM((depth, qkv), bf16),
            pltpu.VMEM(w_out.shape[1:], bf16),
            pltpu.VMEM((rows, qkv), f32),
            pltpu.VMEM((n, rows, qkv), bf16),
            pltpu.VMEM((n, rows, qkv), bf16),
            pltpu.VMEM((rows, GROUP * HD), bf16),
            pltpu.VMEM((n, rows, 2 * HD), bf16),
            pltpu.VMEM((n, 2, half, GROUP * HD), bf16),
            pltpu.VMEM((2, half, w_proj.shape[0]), bf16),
            pltpu.VMEM(w_proj.shape, bf16),
            pltpu.VMEM((rows, n * width), bf16),
            pltpu.VMEM((2 * n, half, width), bf16),
            pltpu.VMEM((n, half, width), bf16),
            pltpu.VMEM((n, half, width), f32),
            pltpu.VMEM((n, 2, half, width), bf16),
            dma((5,)), dma((n, 2)), dma((n,)), dma((n,)), dma((1,)), dma((1,)), dma((n,)), dma((n,)),
            dma((n,)), dma((n,)), dma((n,)), dma((n,)), dma((n,)), dma((n,)),
            dma((n,)), dma((n,)), dma((n,)), dma((n,)), dma((n,)), dma((n,)),
        ],
        compiler_params=pltpu.CompilerParams(
            collective_id=0, has_side_effects=True, vmem_limit_bytes=56 * 1024 * 1024
        ),
    )(
        held[0], text, frames, join, ln_gain[None], w_proj, b_proj[None], norm_gain, w_qkv, b_qkv, w_out
    )
    return out[None]


def section(held, text, frames, join, ln_gain, w_proj, b_proj, norm_gain, w_qkv, b_qkv, w_out):
    segs, n = lax.axis_size("segment"), lax.axis_size("ctx")
    rows, width = held.shape[1], held.shape[2] // n
    args = (held, text, frames, join, ln_gain, w_proj, b_proj, norm_gain, w_qkv, b_qkv, w_out)
    whole_tiles = width % 128 == 0 and rows % 32 == 0 and w_proj.shape[0] % 128 == 0
    if whole_tiles and n * rows <= 1024 and lax.axis_size("tp") == 2:
        return relayed((segs, n, rows, width), *args)
    return on_device(*args)


def solution(mesh):
    return jax.shard_map(
        section,
        mesh=mesh,
        in_specs=(
            P("segment", "ctx", None),
            P("ctx", None),
            P("ctx", None),
            P("ctx"),
            P(),
            P("tp", None),
            P(),
            P(),
            P(None, "ctx", "tp"),
            P(None, "tp"),
            P(None, "tp", "ctx"),
        ),
        out_specs=P("segment", "ctx", None),
        check_vma=False,
    )
```

```python
from functools import partial

import jax
import jax.numpy as jnp
from jax import lax
from jax.experimental import pallas as pl
from jax.experimental.pallas import tpu as pltpu
from jax.sharding import PartitionSpec as P

HD = 128
GROUP = 7
FRAME = 64


def shifted(value, axis, by):
    devices = lax.axis_size(axis)
    pairs = [(i, i + by) for i in range(devices) if 0 <= i + by < devices]
    return lax.ppermute(value, axis, pairs)


def update_state(softmax_state, query_flat, query_pos, keys_in, values_in, offset):
    peak_old, total_old, accum_old = softmax_state
    key_pos = jnp.arange(keys_in.shape[0], dtype=jnp.int32)
    scores = jnp.dot(query_flat, keys_in.T, preferred_element_type=jnp.float32) * HD ** (-0.5)
    allowed = key_pos[None, :] <= query_pos[:, None]
    scores = jnp.where(allowed, scores, -1e30)
    peak_new = jnp.maximum(peak_old, jnp.max(scores, axis=1))
    weights = jnp.where(allowed, jnp.exp(scores - peak_new[:, None]), 0.0)
    total_new = jnp.sum(weights, axis=1)
    accum_new = jnp.dot(weights.astype(jnp.bfloat16), values_in, preferred_element_type=jnp.float32)
    return (peak_new, total_new, accum_new)


def keep_state(softmax_state):
    return softmax_state


def on_device(held, text, frames, join, ln_gain, w_proj, b_proj, norm_gain, w_qkv, b_qkv, w_out):
    segment_id = lax.axis_index("segment")
    ctx_id = lax.axis_index("ctx")
    tp_id = lax.axis_index("tp")
    hidden_in = shifted(held[0], "segment", 1)
    tok_rows = hidden_in.shape[0]
    half_rows = tok_rows // 2
    layer_id = jnp.maximum(segment_id - 1, 0)
    weight_qkv = lax.dynamic_index_in_dim(w_qkv, layer_id, 0, keepdims=False)
    bias_qkv = lax.dynamic_index_in_dim(b_qkv, layer_id, 0, keepdims=False)
    layer_gain = lax.dynamic_index_in_dim(norm_gain, layer_id, 0, keepdims=False)
    weight_out = lax.dynamic_index_in_dim(w_out, layer_id, 0, keepdims=False)
    inputs = hidden_in.astype(jnp.float32)
    normed = (
        inputs * lax.rsqrt(jnp.mean(inputs * inputs, axis=1, keepdims=True) + 1e-06) * layer_gain
    ).astype(jnp.bfloat16)
    merged = jnp.dot(
        normed,
        lax.all_gather(weight_qkv, "ctx", axis=0, tiled=True),
        preferred_element_type=jnp.float32,
    )
    merged = (merged + bias_qkv).astype(jnp.bfloat16)
    query_cols = GROUP * HD
    queries = merged[:, :query_cols]
    key_part = merged[:, query_cols : query_cols + HD]
    value_part = merged[:, query_cols + HD : query_cols + 2 * HD]
    local_steps = jnp.arange(half_rows, dtype=jnp.int32)
    first_pos = ctx_id * tok_rows + local_steps
    second_q = queries[half_rows:]
    second_pos = ctx_id * tok_rows + half_rows + local_steps
    first_flat = queries[:half_rows].reshape(half_rows * GROUP, HD)
    second_flat = second_q.reshape(half_rows * GROUP, HD)
    first_qpos = jnp.repeat(first_pos, GROUP)
    second_qpos = jnp.repeat(second_pos, GROUP)
    flat_rows = half_rows * GROUP
    empty = (
        jnp.full((flat_rows,), -1e30, jnp.float32),
        jnp.zeros((flat_rows,), jnp.float32),
        jnp.zeros((flat_rows, HD), jnp.float32),
    )
    carried = (empty, empty)
    offset = jnp.int32(0)
    keys_in = lax.all_gather(key_part, "ctx", axis=0, tiled=True)
    values_in = lax.all_gather(value_part, "ctx", axis=0, tiled=True)
    updated = []
    for softmax_state, query_flat, query_pos in (
        (carried[0], first_flat, first_qpos),
        (carried[1], second_flat, second_qpos),
    ):
        step_fn = partial(
            update_state,
            query_flat=query_flat,
            query_pos=query_pos,
            keys_in=keys_in,
            values_in=values_in,
            offset=offset,
        )
        updated.append(lax.cond(offset <= jnp.max(query_pos), step_fn, keep_state, softmax_state))

    def finish(softmax_state):
        return (
            (softmax_state[2] / softmax_state[1][:, None])
            .astype(jnp.bfloat16)
            .reshape(half_rows, GROUP * HD)
        )

    first_out = finish(updated[0])
    second_out = finish(updated[1])
    attended = jnp.concatenate([first_out, second_out], axis=0)
    partial_model = jnp.dot(
        attended,
        lax.all_gather(weight_out, "ctx", axis=1, tiled=True),
        preferred_element_type=jnp.float32,
    )
    positions = ctx_id * tok_rows + jnp.arange(tok_rows, dtype=jnp.int32)[:, None]
    starts = join[None, :]
    inside = (positions >= starts) & (positions < starts + FRAME)
    frame_base = (jnp.arange(join.shape[0], dtype=jnp.int32) * FRAME)[None, :]
    source = jnp.sum(jnp.where(inside, frame_base + positions - starts, 0), axis=1)
    is_vision = jnp.any(inside, axis=1)

    def vision_term():
        frame_in = frames.astype(jnp.float32)
        center = jnp.mean(frame_in, axis=1, keepdims=True)
        spread = jnp.mean((frame_in - center) * (frame_in - center), axis=1, keepdims=True)
        normed_frames = ((frame_in - center) * lax.rsqrt(spread + 1e-06) * ln_gain).astype(
            jnp.bfloat16
        )
        vis_width = w_proj.shape[0]
        normed_half = lax.dynamic_slice_in_dim(normed_frames, tp_id * vis_width, vis_width, 1)
        projected = jnp.dot(normed_half, w_proj, preferred_element_type=jnp.float32)
        return jnp.where(is_vision[:, None], jnp.take(projected, source, axis=0), 0.0)

    def model_term():
        return partial_model

    is_first = segment_id == 0
    section_term = lax.cond(is_first, vision_term, model_term)
    baseline = jnp.where(
        is_first, jnp.where(is_vision[:, None], b_proj[None, :], text.astype(jnp.float32)), inputs
    )
    summed = lax.psum(section_term.astype(jnp.bfloat16), "tp").astype(jnp.float32)
    result = (baseline + summed).astype(jnp.bfloat16)
    return result[None]


def relay_kernel(
    sizes,
    held, text, frames, join, ln_gain, w_proj, b_proj, norm_gain, w_qkv, b_qkv, w_out,
    out,
    held_v, rs_out, rs_in, x_v, wq_v, wo_v, own_part, part_out, part_in, q_v, kv_v, att_v,
    vis_v, wp_v, text_v, half_out, half_in, half_own, res_out, res_v, both, vis_out, vis_in, vis_own,
    load_sem, store_sem, x_send, x_recv, rs_send, rs_recv, fwd_send, fwd_recv,
    part_send, part_recv, kv_send, kv_recv, att_send, att_recv,
    half_send, half_recv, res_send, res_recv, pair_send, pair_recv, vis_send, vis_recv,
):
    segs, n, rows, width = sizes
    unit = rows // 2
    half = unit // 2
    last = segs - 1
    s = lax.axis_index("segment")
    c = lax.axis_index("ctx")
    t = lax.axis_index("tp")
    owner = jnp.where(s == 0, last, s)
    layer = owner - 1
    runs = (s < last, s > 0)
    feeds = s < last
    query_cols = GROUP * HD

    def remote(src, dst, send, recv, segment, ctx, tp):
        return pltpu.make_async_remote_copy(
            src_ref=src, dst_ref=dst, send_sem=send, recv_sem=recv,
            device_id={"segment": segment, "ctx": ctx, "tp": tp},
            device_id_type=pl.DeviceIdType.MESH,
        )

    def cols(k):
        return pl.ds(pl.multiple_of(k * width, 128), width)

    def strip(r, side):
        return pl.ds(pl.multiple_of(r * unit + side * half, 16), half)

    def turn(d):
        return lax.rem(c + d, n)

    def far_first(i):
        return jnp.where(2 * c < n, n - 1 - i, i)

    loads = {
        "held": pltpu.make_async_copy(held, held_v, load_sem.at[0]),
        "wq": pltpu.make_async_copy(w_qkv.at[layer], wq_v, load_sem.at[1]),
        "wo": pltpu.make_async_copy(w_out.at[layer], wo_v, load_sem.at[2]),
        "wp": pltpu.make_async_copy(w_proj, wp_v, load_sem.at[3]),
        "text": pltpu.make_async_copy(text, text_v, load_sem.at[4]),
    }
    barrier = pltpu.get_barrier_semaphore()

    def greet(segment, ctx, tp):
        pl.semaphore_signal(
            barrier, inc=1, device_id={"segment": segment, "ctx": ctx, "tp": tp},
            device_id_type=pl.DeviceIdType.MESH,
        )

    greet(s, c, 1 - t)
    for d in range(1, n):
        greet(s, turn(d), t)
    for e in range(1, segs):
        for d in range(n):
            greet(lax.rem(s + e, segs), turn(d), t)

    @pl.when(feeds)
    def _():
        loads["held"].start()

    loads["wq"].start()
    loads["wo"].start()

    @pl.when(s == 0)
    def _():
        loads["wp"].start()
        loads["text"].start()

    for k in range(n):
        @pl.when(k > c)
        def _():
            kv_v[k] = jnp.zeros((2, unit, 2 * HD), jnp.bfloat16)

    kv_v[c, 1] = jnp.zeros((unit, 2 * HD), jnp.bfloat16)

    pl.semaphore_wait(barrier, segs * n)

    def x_copy(r, k):
        worker = jnp.where(s == last - 1, 0, s + 1) if r == 0 else jnp.minimum(s + 1, last)
        return remote(
            held.at[strip(r, t), cols(k)], x_v.at[c, r, t],
            x_send.at[r, k], x_recv.at[r, c], worker, k, t,
        )

    def rs_copy(to, slot):
        return remote(rs_out, rs_in, rs_send.at[slot], rs_recv.at[0], to, c, t)

    def fwd_copy(r, j, side):
        return remote(
            x_v.at[j, r, side], x_v.at[j, r, side], fwd_send.at[r, j], fwd_recv.at[r, j],
            s, c, 1 - t,
        )

    def part_copy(r, k, to, slot):
        return remote(
            part_out.at[r, k], part_in.at[r, slot], part_send.at[r, k], part_recv.at[r, slot],
            s, to, t,
        )

    def part_wait(r, slot):
        part_copy(r, c, turn(1), slot).wait_recv()

    def send_part(r, k):
        @pl.when(k > c)
        def _():
            part_copy(r, k, jnp.minimum(c + 1, n - 1), k).start()

        @pl.when(k < c)
        def _():
            to = jnp.maximum(c - 1, 0)
            part_copy(r, k, to, jnp.where(k == to, n, k)).start()

    def kv_copy(r, to, k, slot, side):
        return remote(
            kv_v.at[slot, r], kv_v.at[slot, r], kv_send.at[r, side, k], kv_recv.at[r, slot],
            to, k, t,
        )

    def att_copy(r, k, slot):
        return remote(
            att_v.at[slot, r], att_v.at[slot, r], att_send.at[r, k], att_recv.at[r, slot], s, k, t
        )

    def half_copy(r, j):
        return remote(
            half_out.at[r, j], half_in.at[r, j], half_send.at[r, j], half_recv.at[r, j],
            s, c, 1 - t,
        )

    def vis_copy(k):
        return remote(vis_out.at[k], vis_in.at[k], vis_send.at[k], vis_recv.at[k], s, c, 1 - t)

    def res_copy(r, j, slot):
        return remote(
            res_out.at[r, j], res_v.at[slot, r, t], res_send.at[r, j], res_recv.at[r, slot],
            owner, j, t,
        )

    def pair_copy(r, k, side):
        return remote(
            res_v.at[k, r, side], res_v.at[k, r, side], pair_send.at[r, k], pair_recv.at[r, k],
            s, c, 1 - t,
        )

    def out_copy(r, k, side):
        return pltpu.make_async_copy(
            res_v.at[k, r, side], out.at[strip(r, side), cols(k)], store_sem.at[r, k, side]
        )

    @pl.when(feeds)
    def _():
        for r in range(2):
            for d in range(n):
                x_copy(r, turn(d)).start()
        loads["held"].wait()

        @pl.loop(0, rows // 32)
        def _(i):
            at = pl.ds(pl.multiple_of(i * 32, 32), 32)
            x = held_v[at, :].astype(jnp.float32)
            scale = lax.rsqrt(jnp.mean(x * x, axis=1, keepdims=True) + 1e-06)
            rs_out[at, :] = jnp.broadcast_to(scale, (32, HD))

        rs_copy(s + 1, 0).start()

        @pl.when(s == last - 1)
        def _():
            rs_copy(0, 1).start()

    loads["wq"].wait()
    gain = norm_gain[pl.ds(layer, 1), cols(c)]
    bias = b_qkv[pl.ds(layer, 1), :]

    for r in range(2):
        @pl.when(runs[r])
        def _():
            @pl.loop(0, n)
            def _(d):
                j = turn(d)
                remote(
                    x_v.at[j, r, t], x_v.at[j, r, t], x_send.at[r, j], x_recv.at[r, j],
                    s, c, 1 - t,
                ).wait_recv()
                fwd_copy(r, j, t).start()

    for r in range(2):
        @pl.when(runs[r])
        def _():
            @pl.loop(0, n)
            def _(i):
                j = far_first(i)
                fwd_copy(r, j, 1 - t).wait_recv()
                x = x_v[j, r].reshape(unit, width).astype(jnp.float32)
                product = jnp.dot(
                    (x * gain).astype(jnp.bfloat16), wq_v[...], preferred_element_type=jnp.float32
                )
                own_part[r, j] = product

                @pl.when(((c == 0) | (c == n - 1)) & (j != c))
                def _():
                    part_out[r, j] = product.astype(jnp.bfloat16)
                    send_part(r, j)

    @pl.when(s == 0)
    def _():
        frame_in = frames[...].astype(jnp.float32)
        center = jnp.mean(frame_in, axis=1, keepdims=True)
        spread = jnp.mean((frame_in - center) * (frame_in - center), axis=1, keepdims=True)
        normed = ((frame_in - center) * lax.rsqrt(spread + 1e-06) * ln_gain[...]).astype(
            jnp.bfloat16
        )
        vis_width = w_proj.shape[0]
        normed = jnp.where(t == 0, normed[:, :vis_width], normed[:, vis_width:])
        count = frames.shape[0]
        token = lax.broadcasted_iota(jnp.int32, (unit, count), 1)
        row = lax.broadcasted_iota(jnp.int32, (unit, count), 0)
        row = jnp.where(row < half, row, row + half)
        for side in range(2):
            position = c * rows + side * half + row
            pick = jnp.zeros((unit, count), jnp.float32)
            for f in range(count // FRAME):
                mine = (token >= f * FRAME) & (token < (f + 1) * FRAME)
                hit = mine & (position - join[f] == token - f * FRAME)
                pick = jnp.where(hit, 1.0, pick)
            vis_v[side] = jnp.dot(
                pick.astype(jnp.bfloat16), normed, preferred_element_type=jnp.float32
            ).astype(jnp.bfloat16)
        loads["wp"].wait()
        loads["text"].wait()

        @pl.loop(0, n)
        def _(k):
            vis_out[k] = jnp.dot(
                vis_v[1 - t], wp_v[:, cols(k)], preferred_element_type=jnp.float32
            ).astype(jnp.bfloat16)
            vis_copy(k).start()
            vis_own[k] = jnp.dot(vis_v[t], wp_v[:, cols(k)], preferred_element_type=jnp.float32)

    def pass_parts(r):
        @pl.when(runs[r] & (c > 0) & (c < n - 1))
        def _():
            @pl.loop(0, n)
            def _(i):
                j = far_first(i)

                @pl.when(j != c)
                def _():
                    part_wait(r, j)
                    part_out[r, j] = (
                        own_part[r, j] + part_in[r, j].astype(jnp.float32)
                    ).astype(jnp.bfloat16)
                    send_part(r, j)

    def merge(r):
        @pl.when(runs[r])
        def _():
            @pl.when(c > 0)
            def _():
                part_wait(r, c)
                own_part[r, c] += part_in[r, c].astype(jnp.float32)

            @pl.when(c < n - 1)
            def _():
                part_wait(r, n)
                own_part[r, c] += part_in[r, n].astype(jnp.float32)

            scale = rs_in[r * unit : (r + 1) * unit, :1]
            merged = (own_part[r, c] * scale + bias).astype(jnp.bfloat16)
            q_v[r] = merged[:, :query_cols]
            kv_v[c, r] = merged[:, query_cols:]
            for k in range(n):
                @pl.when(k > c)
                def _():
                    kv_copy(r, s, k, c, 0).start()

                @pl.when((k > c) & (owner == last))
                def _():
                    kv_copy(r, last - s, k, c, 1).start()

            if r == 0:
                @pl.when(s == 0)
                def _():
                    kv_copy(0, last, c, c, 1).start()

    def attend(r):
        @pl.when(runs[r])
        def _():
            take = (s < last) if r == 0 else (s == last)
            for k in range(n):
                @pl.when((k < c) & take)
                def _():
                    for part in range(2):
                        kv_copy(part, s, turn(1), k, 0).wait_recv()

            if r == 1:
                @pl.when(s == last)
                def _():
                    kv_copy(0, s, turn(1), c, 0).wait_recv()

            first = c * rows + r * unit
            query_pos = first + lax.broadcasted_iota(jnp.int32, (unit, n * rows), 0)
            allowed = lax.broadcasted_iota(jnp.int32, (unit, n * rows), 1) <= query_pos
            keys = kv_v[:, :, :, :HD].reshape(n * rows, HD)
            values = kv_v[:, :, :, HD:].reshape(n * rows, HD)
            for h in range(GROUP):
                q = q_v[r, :, h * HD : (h + 1) * HD]
                scores = lax.dot_general(
                    q, keys, (((1,), (1,)), ((), ())), preferred_element_type=jnp.float32
                ) * HD ** (-0.5)
                scores = jnp.where(allowed, scores, -1e30)
                weights = jnp.exp(scores - jnp.max(scores, axis=1, keepdims=True))
                total = jnp.sum(weights, axis=1, keepdims=True)
                mixed = jnp.dot(
                    weights.astype(jnp.bfloat16), values, preferred_element_type=jnp.float32
                ) / total
                att_v[c, r, :, h * HD : (h + 1) * HD] = mixed.astype(jnp.bfloat16)
            for d in range(1, n):
                att_copy(r, turn(d), c).start()

    pass_parts(0)
    remote(rs_out, rs_in, rs_send.at[0], rs_recv.at[0], s, c, 1 - t).wait_recv()
    merge(0)
    pass_parts(1)
    merge(1)
    attend(0)
    attend(1)

    @pl.when(s == 0)
    def _():
        row = lax.broadcasted_iota(jnp.int32, (half, width), 0)

        @pl.loop(0, n)
        def _(k):
            vis_copy(k).wait_recv()
            total = vis_own[k] + vis_in[k].astype(jnp.float32) + b_proj[:, cols(k)]
            for r in range(2):
                place = c * rows + r * unit + t * half + row
                inside = jnp.zeros((half, width), jnp.bool_)
                for f in range(frames.shape[0] // FRAME):
                    inside = inside | ((place >= join[f]) & (place < join[f] + FRAME))
                base = text_v[strip(r, t), cols(k)].astype(jnp.float32)
                res_v[k, r, t] = jnp.where(
                    inside, total[r * half : (r + 1) * half], base
                ).astype(jnp.bfloat16)
                pair_copy(r, k, t).start()
                out_copy(r, k, t).start()

    loads["wo"].wait()
    for r in range(2):
        @pl.when(runs[r])
        def _():
            @pl.loop(0, n)
            def _(d):
                j = turn(d)

                @pl.when(d > 0)
                def _():
                    att_copy(r, j, j).wait_recv()

                both[...] = jnp.dot(
                    att_v[j, r], wo_v[...], preferred_element_type=jnp.float32
                ).reshape(2, half, width)
                half_out[r, j] = both[1 - t].astype(jnp.bfloat16)
                half_copy(r, j).start()
                half_own[r, j] = x_v[j, r, t].astype(jnp.float32) + both[t]

    for r in range(2):
        @pl.when(runs[r])
        def _():
            @pl.loop(0, n)
            def _(d):
                j = turn(d)
                half_copy(r, j).wait_recv()
                total = (half_own[r, j] + half_in[r, j].astype(jnp.float32)).astype(jnp.bfloat16)

                @pl.when((d == 0) & (s > 0))
                def _():
                    res_v[c, r, t] = total
                    pair_copy(r, c, t).start()
                    out_copy(r, c, t).start()

                @pl.when((d > 0) | (s == 0))
                def _():
                    res_out[r, j] = total
                    res_copy(r, j, c).start()

    for r in range(2):
        @pl.when(s > 0)
        def _():
            @pl.loop(0, n)
            def _(d):
                k = turn(d)

                @pl.when((d > 0) | ((s == last) & (r == 0)))
                def _():
                    remote(
                        res_out.at[r, k], res_v.at[k, r, t], res_send.at[r, k], res_recv.at[r, k],
                        s, c, 1 - t,
                    ).wait_recv()
                    pair_copy(r, k, t).start()
                    out_copy(r, k, t).start()

    for r in range(2):
        @pl.loop(0, n)
        def _(d):
            k = turn(d)
            pair_copy(r, k, 1 - t).wait_recv()
            out_copy(r, k, 1 - t).start()

    @pl.when(feeds)
    def _():
        for r in range(2):
            for k in range(n):
                x_copy(r, k).wait_send()
        rs_copy(s + 1, 0).wait_send()

        @pl.when(s == last - 1)
        def _():
            rs_copy(0, 1).wait_send()

    @pl.when(s == 0)
    def _():
        kv_copy(0, last, c, c, 1).wait_send()
        for k in range(n):
            vis_copy(k).wait_send()

    for r in range(2):
        @pl.when(runs[r])
        def _():
            @pl.loop(0, n)
            def _(d):
                j = turn(d)
                fwd_copy(r, j, t).wait_send()
                half_copy(r, j).wait_send()

                @pl.when(d > 0)
                def _():
                    part_copy(r, j, turn(1), c).wait_send()
                    att_copy(r, j, c).wait_send()

                @pl.when((d > 0) | (s == 0))
                def _():
                    res_copy(r, j, c).wait_send()

                @pl.when(j > c)
                def _():
                    kv_copy(r, s, j, c, 0).wait_send()

                @pl.when((j > c) & (owner == last))
                def _():
                    kv_copy(r, last - s, j, c, 1).wait_send()

        @pl.loop(0, n)
        def _(k):
            pair_copy(r, k, t).wait_send()
            out_copy(r, k, 0).wait()
            out_copy(r, k, 1).wait()


def relayed(sizes, held, text, frames, join, ln_gain, w_proj, b_proj, norm_gain, w_qkv, b_qkv, w_out):
    segs, n, rows, width = sizes
    unit = rows // 2
    half = unit // 2
    depth, qkv = w_qkv.shape[1:]
    bf16, f32 = jnp.bfloat16, jnp.float32
    hbm = pl.BlockSpec(memory_space=pl.ANY)
    vmem = pl.BlockSpec(memory_space=pltpu.VMEM)
    smem = pl.BlockSpec(memory_space=pltpu.SMEM)
    dma = pltpu.SemaphoreType.DMA
    out = pl.pallas_call(
        partial(relay_kernel, sizes),
        out_shape=jax.ShapeDtypeStruct((rows, n * width), bf16),
        in_specs=[hbm, hbm, vmem, smem, vmem, hbm, vmem, vmem, hbm, vmem, hbm],
        out_specs=hbm,
        scratch_shapes=[
            pltpu.VMEM((rows, n * width), bf16),
            pltpu.VMEM((rows, HD), f32),
            pltpu.VMEM((rows, HD), f32),
            pltpu.VMEM((n, 2, 2, half, width), bf16),
            pltpu.VMEM((depth, qkv), bf16),
            pltpu.VMEM(w_out.shape[1:], bf16),
            pltpu.VMEM((2, n, unit, qkv), f32),
            pltpu.VMEM((2, n, unit, qkv), bf16),
            pltpu.VMEM((2, n + 1, unit, qkv), bf16),
            pltpu.VMEM((2, unit, GROUP * HD), bf16),
            pltpu.VMEM((n, 2, unit, 2 * HD), bf16),
            pltpu.VMEM((n, 2, unit, GROUP * HD), bf16),
            pltpu.VMEM((2, unit, w_proj.shape[0]), bf16),
            pltpu.VMEM(w_proj.shape, bf16),
            pltpu.VMEM((rows, n * width), bf16),
            pltpu.VMEM((2, n, half, width), bf16),
            pltpu.VMEM((2, n, half, width), bf16),
            pltpu.VMEM((2, n, half, width), f32),
            pltpu.VMEM((2, n, half, width), bf16),
            pltpu.VMEM((n, 2, 2, half, width), bf16),
            pltpu.VMEM((2, half, width), f32),
            pltpu.VMEM((n, unit, width), bf16),
            pltpu.VMEM((n, unit, width), bf16),
            pltpu.VMEM((n, unit, width), f32),
            dma((5,)), dma((2, n, 2)), dma((2, n)), dma((2, n)), dma((2,)), dma((1,)),
            dma((2, n)), dma((2, n)), dma((2, n)), dma((2, n + 1)), dma((2, 2, n)), dma((2, n)),
            dma((2, n)), dma((2, n)), dma((2, n)), dma((2, n)), dma((2, n)), dma((2, n)),
            dma((2, n)), dma((2, n)), dma((n,)), dma((n,)),
        ],
        compiler_params=pltpu.CompilerParams(
            collective_id=0, has_side_effects=True, vmem_limit_bytes=60 * 1024 * 1024
        ),
    )(
        held[0], text, frames, join, ln_gain[None], w_proj, b_proj[None], norm_gain, w_qkv, b_qkv, w_out
    )
    return out[None]


def section(held, text, frames, join, ln_gain, w_proj, b_proj, norm_gain, w_qkv, b_qkv, w_out):
    segs, n = lax.axis_size("segment"), lax.axis_size("ctx")
    rows, width = held.shape[1], held.shape[2] // n
    args = (held, text, frames, join, ln_gain, w_proj, b_proj, norm_gain, w_qkv, b_qkv, w_out)
    whole_tiles = width % 128 == 0 and rows % 64 == 0 and w_proj.shape[0] % 128 == 0
    if whole_tiles and n * rows <= 1024 and lax.axis_size("tp") == 2 and segs > 2:
        return relayed((segs, n, rows, width), *args)
    return on_device(*args)


def solution(mesh):
    return jax.shard_map(
        section,
        mesh=mesh,
        in_specs=(
            P("segment", "ctx", None),
            P("ctx", None),
            P("ctx", None),
            P("ctx"),
            P(),
            P("tp", None),
            P(),
            P(),
            P(None, "ctx", "tp"),
            P(None, "tp"),
            P(None, "tp", "ctx"),
        ),
        out_specs=P("segment", "ctx", None),
        check_vma=False,
    )
```

```python
from functools import partial

import jax
import jax.numpy as jnp
from jax import lax
from jax.experimental import pallas as pl
from jax.experimental.pallas import tpu as pltpu
from jax.sharding import PartitionSpec as P

HD = 128
GROUP = 7
FRAME = 64


def shifted(value, axis, by):
    devices = lax.axis_size(axis)
    pairs = [(i, i + by) for i in range(devices) if 0 <= i + by < devices]
    return lax.ppermute(value, axis, pairs)


def update_state(softmax_state, query_flat, query_pos, keys_in, values_in, offset):
    peak_old, total_old, accum_old = softmax_state
    key_pos = jnp.arange(keys_in.shape[0], dtype=jnp.int32)
    scores = jnp.dot(query_flat, keys_in.T, preferred_element_type=jnp.float32) * HD ** (-0.5)
    allowed = key_pos[None, :] <= query_pos[:, None]
    scores = jnp.where(allowed, scores, -1e30)
    peak_new = jnp.maximum(peak_old, jnp.max(scores, axis=1))
    weights = jnp.where(allowed, jnp.exp(scores - peak_new[:, None]), 0.0)
    total_new = jnp.sum(weights, axis=1)
    accum_new = jnp.dot(weights.astype(jnp.bfloat16), values_in, preferred_element_type=jnp.float32)
    return (peak_new, total_new, accum_new)


def keep_state(softmax_state):
    return softmax_state


def on_device(held, text, frames, join, ln_gain, w_proj, b_proj, norm_gain, w_qkv, b_qkv, w_out):
    segment_id = lax.axis_index("segment")
    ctx_id = lax.axis_index("ctx")
    tp_id = lax.axis_index("tp")
    hidden_in = shifted(held[0], "segment", 1)
    tok_rows = hidden_in.shape[0]
    half_rows = tok_rows // 2
    layer_id = jnp.maximum(segment_id - 1, 0)
    weight_qkv = lax.dynamic_index_in_dim(w_qkv, layer_id, 0, keepdims=False)
    bias_qkv = lax.dynamic_index_in_dim(b_qkv, layer_id, 0, keepdims=False)
    layer_gain = lax.dynamic_index_in_dim(norm_gain, layer_id, 0, keepdims=False)
    weight_out = lax.dynamic_index_in_dim(w_out, layer_id, 0, keepdims=False)
    inputs = hidden_in.astype(jnp.float32)
    normed = (
        inputs * lax.rsqrt(jnp.mean(inputs * inputs, axis=1, keepdims=True) + 1e-06) * layer_gain
    ).astype(jnp.bfloat16)
    merged = jnp.dot(
        normed,
        lax.all_gather(weight_qkv, "ctx", axis=0, tiled=True),
        preferred_element_type=jnp.float32,
    )
    merged = (merged + bias_qkv).astype(jnp.bfloat16)
    query_cols = GROUP * HD
    queries = merged[:, :query_cols]
    key_part = merged[:, query_cols : query_cols + HD]
    value_part = merged[:, query_cols + HD : query_cols + 2 * HD]
    local_steps = jnp.arange(half_rows, dtype=jnp.int32)
    first_pos = ctx_id * tok_rows + local_steps
    second_q = queries[half_rows:]
    second_pos = ctx_id * tok_rows + half_rows + local_steps
    first_flat = queries[:half_rows].reshape(half_rows * GROUP, HD)
    second_flat = second_q.reshape(half_rows * GROUP, HD)
    first_qpos = jnp.repeat(first_pos, GROUP)
    second_qpos = jnp.repeat(second_pos, GROUP)
    flat_rows = half_rows * GROUP
    empty = (
        jnp.full((flat_rows,), -1e30, jnp.float32),
        jnp.zeros((flat_rows,), jnp.float32),
        jnp.zeros((flat_rows, HD), jnp.float32),
    )
    carried = (empty, empty)
    offset = jnp.int32(0)
    keys_in = lax.all_gather(key_part, "ctx", axis=0, tiled=True)
    values_in = lax.all_gather(value_part, "ctx", axis=0, tiled=True)
    updated = []
    for softmax_state, query_flat, query_pos in (
        (carried[0], first_flat, first_qpos),
        (carried[1], second_flat, second_qpos),
    ):
        step_fn = partial(
            update_state,
            query_flat=query_flat,
            query_pos=query_pos,
            keys_in=keys_in,
            values_in=values_in,
            offset=offset,
        )
        updated.append(lax.cond(offset <= jnp.max(query_pos), step_fn, keep_state, softmax_state))

    def finish(softmax_state):
        return (
            (softmax_state[2] / softmax_state[1][:, None])
            .astype(jnp.bfloat16)
            .reshape(half_rows, GROUP * HD)
        )

    first_out = finish(updated[0])
    second_out = finish(updated[1])
    attended = jnp.concatenate([first_out, second_out], axis=0)
    partial_model = jnp.dot(
        attended,
        lax.all_gather(weight_out, "ctx", axis=1, tiled=True),
        preferred_element_type=jnp.float32,
    )
    positions = ctx_id * tok_rows + jnp.arange(tok_rows, dtype=jnp.int32)[:, None]
    starts = join[None, :]
    inside = (positions >= starts) & (positions < starts + FRAME)
    frame_base = (jnp.arange(join.shape[0], dtype=jnp.int32) * FRAME)[None, :]
    source = jnp.sum(jnp.where(inside, frame_base + positions - starts, 0), axis=1)
    is_vision = jnp.any(inside, axis=1)

    def vision_term():
        frame_in = frames.astype(jnp.float32)
        center = jnp.mean(frame_in, axis=1, keepdims=True)
        spread = jnp.mean((frame_in - center) * (frame_in - center), axis=1, keepdims=True)
        normed_frames = ((frame_in - center) * lax.rsqrt(spread + 1e-06) * ln_gain).astype(
            jnp.bfloat16
        )
        vis_width = w_proj.shape[0]
        normed_half = lax.dynamic_slice_in_dim(normed_frames, tp_id * vis_width, vis_width, 1)
        projected = jnp.dot(normed_half, w_proj, preferred_element_type=jnp.float32)
        return jnp.where(is_vision[:, None], jnp.take(projected, source, axis=0), 0.0)

    def model_term():
        return partial_model

    is_first = segment_id == 0
    section_term = lax.cond(is_first, vision_term, model_term)
    baseline = jnp.where(
        is_first, jnp.where(is_vision[:, None], b_proj[None, :], text.astype(jnp.float32)), inputs
    )
    summed = lax.psum(section_term.astype(jnp.bfloat16), "tp").astype(jnp.float32)
    result = (baseline + summed).astype(jnp.bfloat16)
    return result[None]


def relay_kernel(
    sizes,
    held, text, frames, join, ln_gain, w_proj, b_proj, norm_gain, w_qkv, b_qkv, w_out,
    out,
    held_v, rs_out, rs_in, x_v, wq_v, wo_v, own_part, part_out, part_in, q_v, kv_v, att_v,
    vis_v, wp_v, text_v, half_out, half_in, half_own, res_out, res_v, both, vis_out, vis_in, vis_own,
    load_sem, store_sem, x_send, x_recv, rs_send, rs_recv, fwd_send, fwd_recv,
    part_send, part_recv, kv_send, kv_recv, att_send, att_recv,
    half_send, half_recv, res_send, res_recv, pair_send, pair_recv, vis_send, vis_recv,
):
    segs, n, rows, width = sizes
    unit = rows // 2
    half = unit // 2
    last = segs - 1
    s = lax.axis_index("segment")
    c = lax.axis_index("ctx")
    t = lax.axis_index("tp")
    owner = jnp.where(s == 0, last, s)
    layer = owner - 1
    runs = (s < last, s > 0)
    feeds = s < last
    query_cols = GROUP * HD

    def remote(src, dst, send, recv, segment, ctx, tp):
        return pltpu.make_async_remote_copy(
            src_ref=src, dst_ref=dst, send_sem=send, recv_sem=recv,
            device_id={"segment": segment, "ctx": ctx, "tp": tp},
            device_id_type=pl.DeviceIdType.MESH,
        )

    def cols(k):
        return pl.ds(pl.multiple_of(k * width, 128), width)

    def strip(r, side):
        return pl.ds(pl.multiple_of(r * unit + side * half, 16), half)

    def turn(d):
        return lax.rem(c + d, n)

    def far_first(i):
        return jnp.where(2 * c < n, n - 1 - i, i)

    def near_first(i):
        return jnp.where(2 * c < n, i, n - 1 - i)

    loads = {
        "held": pltpu.make_async_copy(held, held_v, load_sem.at[0]),
        "wq": pltpu.make_async_copy(w_qkv.at[layer], wq_v, load_sem.at[1]),
        "wo": pltpu.make_async_copy(w_out.at[layer], wo_v, load_sem.at[2]),
        "wp": pltpu.make_async_copy(w_proj, wp_v, load_sem.at[3]),
        "text": pltpu.make_async_copy(text, text_v, load_sem.at[4]),
    }
    barrier = pltpu.get_barrier_semaphore()

    def greet(segment, ctx, tp):
        pl.semaphore_signal(
            barrier, inc=1, device_id={"segment": segment, "ctx": ctx, "tp": tp},
            device_id_type=pl.DeviceIdType.MESH,
        )

    greet(s, c, 1 - t)
    for d in range(1, n):
        greet(s, turn(d), t)
    for e in range(1, segs):
        for d in range(n):
            greet(lax.rem(s + e, segs), turn(d), t)

    @pl.when(feeds)
    def _():
        loads["held"].start()

    loads["wq"].start()
    loads["wo"].start()

    @pl.when(s == 0)
    def _():
        loads["wp"].start()
        loads["text"].start()

    for k in range(n):
        @pl.when(k > c)
        def _():
            kv_v[k] = jnp.zeros((2, unit, 2 * HD), jnp.bfloat16)

    kv_v[c, 1] = jnp.zeros((unit, 2 * HD), jnp.bfloat16)

    pl.semaphore_wait(barrier, segs * n)

    def x_copy(r, k):
        worker = jnp.where(s == last - 1, 0, s + 1) if r == 0 else jnp.minimum(s + 1, last)
        return remote(
            held.at[strip(r, t), cols(k)], x_v.at[c, r, t],
            x_send.at[r, k], x_recv.at[r, c], worker, k, t,
        )

    def rs_copy(to, slot):
        return remote(rs_out, rs_in, rs_send.at[slot], rs_recv.at[0], to, c, t)

    def fwd_copy(r, j, side):
        return remote(
            x_v.at[j, r, side], x_v.at[j, r, side], fwd_send.at[r, j], fwd_recv.at[r, j],
            s, c, 1 - t,
        )

    def part_copy(r, k, to, slot):
        return remote(
            part_out.at[r, k], part_in.at[r, slot], part_send.at[r, k], part_recv.at[r, slot],
            s, to, t,
        )

    def part_wait(r, slot):
        part_copy(r, c, turn(1), slot).wait_recv()

    def send_part(r, k):
        @pl.when(k > c)
        def _():
            part_copy(r, k, jnp.minimum(c + 1, n - 1), k).start()

        @pl.when(k < c)
        def _():
            to = jnp.maximum(c - 1, 0)
            part_copy(r, k, to, jnp.where(k == to, n, k)).start()

    def kv_copy(r, to, k, slot, side):
        return remote(
            kv_v.at[slot, r], kv_v.at[slot, r], kv_send.at[r, side, k], kv_recv.at[r, slot],
            to, k, t,
        )

    def att_copy(r, to, slot, sem):
        return remote(
            att_v.at[slot, r], att_v.at[slot, r], att_send.at[r, sem], att_recv.at[r, slot],
            s, to, t,
        )

    up, down = jnp.minimum(c + 1, n - 1), jnp.maximum(c - 1, 0)

    def each_hop(r, j, act):
        @pl.when((j <= c) & (c < n - 1))
        def _():
            act(att_copy(r, up, j, j))

        @pl.when((j == c) & (c > 0))
        def _():
            act(att_copy(r, down, j, n))

        @pl.when((j > c) & (c > 0))
        def _():
            act(att_copy(r, down, j, j))

    def half_copy(r, j):
        return remote(
            half_out.at[r, j], half_in.at[r, j], half_send.at[r, j], half_recv.at[r, j],
            s, c, 1 - t,
        )

    def vis_copy(k):
        return remote(vis_out.at[k], vis_in.at[k], vis_send.at[k], vis_recv.at[k], s, c, 1 - t)

    def res_copy(r, j, slot):
        return remote(
            res_out.at[r, j], res_v.at[slot, r, t], res_send.at[r, j], res_recv.at[r, slot],
            owner, j, t,
        )

    def pair_copy(r, k, side):
        return remote(
            res_v.at[k, r, side], res_v.at[k, r, side], pair_send.at[r, k], pair_recv.at[r, k],
            s, c, 1 - t,
        )

    def out_copy(r, k, side):
        return pltpu.make_async_copy(
            res_v.at[k, r, side], out.at[strip(r, side), cols(k)], store_sem.at[r, k, side]
        )

    @pl.when(feeds)
    def _():
        for r in range(2):
            for d in range(n):
                x_copy(r, turn(d)).start()
        loads["held"].wait()

        @pl.loop(0, rows // 32)
        def _(i):
            at = pl.ds(pl.multiple_of(i * 32, 32), 32)
            x = held_v[at, :].astype(jnp.float32)
            scale = lax.rsqrt(jnp.mean(x * x, axis=1, keepdims=True) + 1e-06)
            rs_out[at, :] = jnp.broadcast_to(scale, (32, HD))

        rs_copy(s + 1, 0).start()

        @pl.when(s == last - 1)
        def _():
            rs_copy(0, 1).start()

    loads["wq"].wait()
    gain = norm_gain[pl.ds(layer, 1), cols(c)]
    bias = b_qkv[pl.ds(layer, 1), :]

    def hand_over(r, i):
        @pl.when(runs[r])
        def _():
            j = turn(i)
            remote(
                x_v.at[j, r, t], x_v.at[j, r, t], x_send.at[r, j], x_recv.at[r, j], s, c, 1 - t
            ).wait_recv()
            fwd_copy(r, j, t).start()

    def multiply(r, i):
        @pl.when(runs[r])
        def _():
            j = far_first(i)
            fwd_copy(r, j, 1 - t).wait_recv()
            x = x_v[j, r].reshape(unit, width).astype(jnp.float32)
            product = jnp.dot(
                (x * gain).astype(jnp.bfloat16), wq_v[...], preferred_element_type=jnp.float32
            )
            own_part[r, j] = product

            @pl.when(((c == 0) | (c == n - 1)) & (j != c))
            def _():
                part_out[r, j] = product.astype(jnp.bfloat16)
                send_part(r, j)

    def pass_part(r, i):
        j = far_first(i)

        @pl.when(runs[r] & (c > 0) & (c < n - 1) & (j != c))
        def _():
            part_wait(r, j)
            part_out[r, j] = (
                own_part[r, j] + part_in[r, j].astype(jnp.float32)
            ).astype(jnp.bfloat16)
            send_part(r, j)

    @pl.loop(0, n)
    def _(i):
        hand_over(0, i)

    @pl.loop(0, n)
    def _(i):
        multiply(0, i)
        hand_over(1, i)

    @pl.when(s == 0)
    def _():
        frame_in = frames[...].astype(jnp.float32)
        center = jnp.mean(frame_in, axis=1, keepdims=True)
        spread = jnp.mean((frame_in - center) * (frame_in - center), axis=1, keepdims=True)
        normed = ((frame_in - center) * lax.rsqrt(spread + 1e-06) * ln_gain[...]).astype(
            jnp.bfloat16
        )
        vis_width = w_proj.shape[0]
        normed = jnp.where(t == 0, normed[:, :vis_width], normed[:, vis_width:])
        count = frames.shape[0]
        token = lax.broadcasted_iota(jnp.int32, (unit, count), 1)
        row = lax.broadcasted_iota(jnp.int32, (unit, count), 0)
        row = jnp.where(row < half, row, row + half)
        for side in range(2):
            position = c * rows + side * half + row
            pick = jnp.zeros((unit, count), jnp.float32)
            for f in range(count // FRAME):
                mine = (token >= f * FRAME) & (token < (f + 1) * FRAME)
                hit = mine & (position - join[f] == token - f * FRAME)
                pick = jnp.where(hit, 1.0, pick)
            vis_v[side] = jnp.dot(
                pick.astype(jnp.bfloat16), normed, preferred_element_type=jnp.float32
            ).astype(jnp.bfloat16)
        loads["wp"].wait()
        loads["text"].wait()

        @pl.loop(0, n)
        def _(k):
            vis_out[k] = jnp.dot(
                vis_v[1 - t], wp_v[:, cols(k)], preferred_element_type=jnp.float32
            ).astype(jnp.bfloat16)
            vis_copy(k).start()
            vis_own[k] = jnp.dot(vis_v[t], wp_v[:, cols(k)], preferred_element_type=jnp.float32)

    @pl.loop(0, n)
    def _(i):
        multiply(1, i)
        pass_part(0, i)

    def merge(r):
        @pl.when(runs[r])
        def _():
            @pl.when(c > 0)
            def _():
                part_wait(r, c)
                own_part[r, c] += part_in[r, c].astype(jnp.float32)

            @pl.when(c < n - 1)
            def _():
                part_wait(r, n)
                own_part[r, c] += part_in[r, n].astype(jnp.float32)

            scale = rs_in[r * unit : (r + 1) * unit, :1]
            merged = (own_part[r, c] * scale + bias).astype(jnp.bfloat16)
            q_v[r] = merged[:, :query_cols]
            kv_v[c, r] = merged[:, query_cols:]
            for k in range(n):
                @pl.when(k > c)
                def _():
                    kv_copy(r, s, k, c, 0).start()

                @pl.when((k > c) & (owner == last))
                def _():
                    kv_copy(r, last - s, k, c, 1).start()

            if r == 0:
                @pl.when(s == 0)
                def _():
                    kv_copy(0, last, c, c, 1).start()

    def attend(r):
        @pl.when(runs[r])
        def _():
            take = (s < last) if r == 0 else (s == last)
            for k in range(n):
                @pl.when((k < c) & take)
                def _():
                    for part in range(2):
                        kv_copy(part, s, turn(1), k, 0).wait_recv()

            if r == 1:
                @pl.when(s == last)
                def _():
                    kv_copy(0, s, turn(1), c, 0).wait_recv()

            first = c * rows + r * unit
            query_pos = first + lax.broadcasted_iota(jnp.int32, (unit, n * rows), 0)
            allowed = lax.broadcasted_iota(jnp.int32, (unit, n * rows), 1) <= query_pos
            keys = kv_v[:, :, :, :HD].reshape(n * rows, HD)
            values = kv_v[:, :, :, HD:].reshape(n * rows, HD)
            for h in range(GROUP):
                q = q_v[r, :, h * HD : (h + 1) * HD]
                scores = lax.dot_general(
                    q, keys, (((1,), (1,)), ((), ())), preferred_element_type=jnp.float32
                ) * HD ** (-0.5)
                scores = jnp.where(allowed, scores, -1e30)
                weights = jnp.exp(scores - jnp.max(scores, axis=1, keepdims=True))
                total = jnp.sum(weights, axis=1, keepdims=True)
                mixed = jnp.dot(
                    weights.astype(jnp.bfloat16), values, preferred_element_type=jnp.float32
                ) / total
                att_v[c, r, :, h * HD : (h + 1) * HD] = mixed.astype(jnp.bfloat16)
            each_hop(r, c, lambda copy: copy.start())

    remote(rs_out, rs_in, rs_send.at[0], rs_recv.at[0], s, c, 1 - t).wait_recv()
    merge(0)

    @pl.loop(0, n)
    def _(i):
        pass_part(1, i)

    merge(1)
    attend(0)
    attend(1)

    @pl.when(s == 0)
    def _():
        row = lax.broadcasted_iota(jnp.int32, (half, width), 0)

        @pl.loop(0, n)
        def _(k):
            vis_copy(k).wait_recv()
            total = vis_own[k] + vis_in[k].astype(jnp.float32) + b_proj[:, cols(k)]
            for r in range(2):
                place = c * rows + r * unit + t * half + row
                inside = jnp.zeros((half, width), jnp.bool_)
                for f in range(frames.shape[0] // FRAME):
                    inside = inside | ((place >= join[f]) & (place < join[f] + FRAME))
                base = text_v[strip(r, t), cols(k)].astype(jnp.float32)
                res_v[k, r, t] = jnp.where(
                    inside, total[r * half : (r + 1) * half], base
                ).astype(jnp.bfloat16)
                pair_copy(r, k, t).start()
                out_copy(r, k, t).start()

    def project(r, i):
        @pl.when(runs[r])
        def _():
            j = near_first(i)

            @pl.when(j != c)
            def _():
                att_copy(r, turn(1), j, j).wait_recv()
                each_hop(r, j, lambda copy: copy.start())

            both[...] = jnp.dot(
                att_v[j, r], wo_v[...], preferred_element_type=jnp.float32
            ).reshape(2, half, width)
            half_out[r, j] = both[1 - t].astype(jnp.bfloat16)
            half_copy(r, j).start()
            half_own[r, j] = x_v[j, r, t].astype(jnp.float32) + both[t]

    def deliver(r, i):
        @pl.when(runs[r])
        def _():
            j = near_first(i)
            half_copy(r, j).wait_recv()
            total = (half_own[r, j] + half_in[r, j].astype(jnp.float32)).astype(jnp.bfloat16)

            @pl.when((j == c) & (s > 0))
            def _():
                res_v[c, r, t] = total
                pair_copy(r, c, t).start()
                out_copy(r, c, t).start()

            @pl.when((j != c) | (s == 0))
            def _():
                res_out[r, j] = total
                res_copy(r, j, c).start()

    def collect(r, i):
        k = near_first(i)

        @pl.when((s > 0) & ((k != c) | ((s == last) & (r == 0))))
        def _():
            remote(
                res_out.at[r, k], res_v.at[k, r, t], res_send.at[r, k], res_recv.at[r, k],
                s, c, 1 - t,
            ).wait_recv()
            pair_copy(r, k, t).start()
            out_copy(r, k, t).start()

    loads["wo"].wait()

    @pl.loop(0, n)
    def _(i):
        project(0, i)

    @pl.loop(0, n)
    def _(i):
        deliver(0, i)
        project(1, i)

    @pl.loop(0, n)
    def _(i):
        deliver(1, i)
        collect(0, i)

    @pl.loop(0, n)
    def _(i):
        collect(1, i)

    for r in range(2):
        @pl.loop(0, n)
        def _(d):
            k = turn(d)
            pair_copy(r, k, 1 - t).wait_recv()
            out_copy(r, k, 1 - t).start()

    @pl.when(feeds)
    def _():
        for r in range(2):
            for k in range(n):
                x_copy(r, k).wait_send()
        rs_copy(s + 1, 0).wait_send()

        @pl.when(s == last - 1)
        def _():
            rs_copy(0, 1).wait_send()

    @pl.when(s == 0)
    def _():
        kv_copy(0, last, c, c, 1).wait_send()
        for k in range(n):
            vis_copy(k).wait_send()

    for r in range(2):
        @pl.when(runs[r])
        def _():
            @pl.loop(0, n)
            def _(d):
                j = turn(d)
                fwd_copy(r, j, t).wait_send()
                half_copy(r, j).wait_send()

                @pl.when(d > 0)
                def _():
                    part_copy(r, j, turn(1), c).wait_send()

                each_hop(r, j, lambda copy: copy.wait_send())

                @pl.when((d > 0) | (s == 0))
                def _():
                    res_copy(r, j, c).wait_send()

                @pl.when(j > c)
                def _():
                    kv_copy(r, s, j, c, 0).wait_send()

                @pl.when((j > c) & (owner == last))
                def _():
                    kv_copy(r, last - s, j, c, 1).wait_send()

        @pl.loop(0, n)
        def _(k):
            pair_copy(r, k, t).wait_send()
            out_copy(r, k, 0).wait()
            out_copy(r, k, 1).wait()


def relayed(sizes, held, text, frames, join, ln_gain, w_proj, b_proj, norm_gain, w_qkv, b_qkv, w_out):
    segs, n, rows, width = sizes
    unit = rows // 2
    half = unit // 2
    depth, qkv = w_qkv.shape[1:]
    bf16, f32 = jnp.bfloat16, jnp.float32
    hbm = pl.BlockSpec(memory_space=pl.ANY)
    vmem = pl.BlockSpec(memory_space=pltpu.VMEM)
    smem = pl.BlockSpec(memory_space=pltpu.SMEM)
    dma = pltpu.SemaphoreType.DMA
    out = pl.pallas_call(
        partial(relay_kernel, sizes),
        out_shape=jax.ShapeDtypeStruct((rows, n * width), bf16),
        in_specs=[hbm, hbm, vmem, smem, vmem, hbm, vmem, vmem, hbm, vmem, hbm],
        out_specs=hbm,
        scratch_shapes=[
            pltpu.VMEM((rows, n * width), bf16),
            pltpu.VMEM((rows, HD), f32),
            pltpu.VMEM((rows, HD), f32),
            pltpu.VMEM((n, 2, 2, half, width), bf16),
            pltpu.VMEM((depth, qkv), bf16),
            pltpu.VMEM(w_out.shape[1:], bf16),
            pltpu.VMEM((2, n, unit, qkv), f32),
            pltpu.VMEM((2, n, unit, qkv), bf16),
            pltpu.VMEM((2, n + 1, unit, qkv), bf16),
            pltpu.VMEM((2, unit, GROUP * HD), bf16),
            pltpu.VMEM((n, 2, unit, 2 * HD), bf16),
            pltpu.VMEM((n, 2, unit, GROUP * HD), bf16),
            pltpu.VMEM((2, unit, w_proj.shape[0]), bf16),
            pltpu.VMEM(w_proj.shape, bf16),
            pltpu.VMEM((rows, n * width), bf16),
            pltpu.VMEM((2, n, half, width), bf16),
            pltpu.VMEM((2, n, half, width), bf16),
            pltpu.VMEM((2, n, half, width), f32),
            pltpu.VMEM((2, n, half, width), bf16),
            pltpu.VMEM((n, 2, 2, half, width), bf16),
            pltpu.VMEM((2, half, width), f32),
            pltpu.VMEM((n, unit, width), bf16),
            pltpu.VMEM((n, unit, width), bf16),
            pltpu.VMEM((n, unit, width), f32),
            dma((5,)), dma((2, n, 2)), dma((2, n)), dma((2, n)), dma((2,)), dma((1,)),
            dma((2, n)), dma((2, n)), dma((2, n)), dma((2, n + 1)), dma((2, 2, n)), dma((2, n)),
            dma((2, n + 1)), dma((2, n)), dma((2, n)), dma((2, n)), dma((2, n)), dma((2, n)),
            dma((2, n)), dma((2, n)), dma((n,)), dma((n,)),
        ],
        compiler_params=pltpu.CompilerParams(
            collective_id=0, has_side_effects=True, vmem_limit_bytes=60 * 1024 * 1024
        ),
    )(
        held[0], text, frames, join, ln_gain[None], w_proj, b_proj[None], norm_gain, w_qkv, b_qkv, w_out
    )
    return out[None]


def section(held, text, frames, join, ln_gain, w_proj, b_proj, norm_gain, w_qkv, b_qkv, w_out):
    segs, n = lax.axis_size("segment"), lax.axis_size("ctx")
    rows, width = held.shape[1], held.shape[2] // n
    args = (held, text, frames, join, ln_gain, w_proj, b_proj, norm_gain, w_qkv, b_qkv, w_out)
    whole_tiles = width % 128 == 0 and rows % 64 == 0 and w_proj.shape[0] % 128 == 0
    if whole_tiles and n * rows <= 1024 and lax.axis_size("tp") == 2 and segs > 2:
        return relayed((segs, n, rows, width), *args)
    return on_device(*args)


def solution(mesh):
    return jax.shard_map(
        section,
        mesh=mesh,
        in_specs=(
            P("segment", "ctx", None),
            P("ctx", None),
            P("ctx", None),
            P("ctx"),
            P(),
            P("tp", None),
            P(),
            P(),
            P(None, "ctx", "tp"),
            P(None, "tp"),
            P(None, "tp", "ctx"),
        ),
        out_specs=P("segment", "ctx", None),
        check_vma=False,
    )
```

```python
from functools import partial

import jax
import jax.numpy as jnp
from jax import lax
from jax.experimental import pallas as pl
from jax.experimental.pallas import tpu as pltpu
from jax.sharding import PartitionSpec as P

HD = 128
GROUP = 7
FRAME = 64


def shifted(value, axis, by):
    devices = lax.axis_size(axis)
    pairs = [(i, i + by) for i in range(devices) if 0 <= i + by < devices]
    return lax.ppermute(value, axis, pairs)


def update_state(softmax_state, query_flat, query_pos, keys_in, values_in, offset):
    peak_old, total_old, accum_old = softmax_state
    key_pos = jnp.arange(keys_in.shape[0], dtype=jnp.int32)
    scores = jnp.dot(query_flat, keys_in.T, preferred_element_type=jnp.float32) * HD ** (-0.5)
    allowed = key_pos[None, :] <= query_pos[:, None]
    scores = jnp.where(allowed, scores, -1e30)
    peak_new = jnp.maximum(peak_old, jnp.max(scores, axis=1))
    weights = jnp.where(allowed, jnp.exp(scores - peak_new[:, None]), 0.0)
    total_new = jnp.sum(weights, axis=1)
    accum_new = jnp.dot(weights.astype(jnp.bfloat16), values_in, preferred_element_type=jnp.float32)
    return (peak_new, total_new, accum_new)


def keep_state(softmax_state):
    return softmax_state


def on_device(held, text, frames, join, ln_gain, w_proj, b_proj, norm_gain, w_qkv, b_qkv, w_out):
    segment_id = lax.axis_index("segment")
    ctx_id = lax.axis_index("ctx")
    tp_id = lax.axis_index("tp")
    hidden_in = shifted(held[0], "segment", 1)
    tok_rows = hidden_in.shape[0]
    half_rows = tok_rows // 2
    layer_id = jnp.maximum(segment_id - 1, 0)
    weight_qkv = lax.dynamic_index_in_dim(w_qkv, layer_id, 0, keepdims=False)
    bias_qkv = lax.dynamic_index_in_dim(b_qkv, layer_id, 0, keepdims=False)
    layer_gain = lax.dynamic_index_in_dim(norm_gain, layer_id, 0, keepdims=False)
    weight_out = lax.dynamic_index_in_dim(w_out, layer_id, 0, keepdims=False)
    inputs = hidden_in.astype(jnp.float32)
    normed = (
        inputs * lax.rsqrt(jnp.mean(inputs * inputs, axis=1, keepdims=True) + 1e-06) * layer_gain
    ).astype(jnp.bfloat16)
    merged = jnp.dot(
        normed,
        lax.all_gather(weight_qkv, "ctx", axis=0, tiled=True),
        preferred_element_type=jnp.float32,
    )
    merged = (merged + bias_qkv).astype(jnp.bfloat16)
    query_cols = GROUP * HD
    queries = merged[:, :query_cols]
    key_part = merged[:, query_cols : query_cols + HD]
    value_part = merged[:, query_cols + HD : query_cols + 2 * HD]
    local_steps = jnp.arange(half_rows, dtype=jnp.int32)
    first_pos = ctx_id * tok_rows + local_steps
    second_q = queries[half_rows:]
    second_pos = ctx_id * tok_rows + half_rows + local_steps
    first_flat = queries[:half_rows].reshape(half_rows * GROUP, HD)
    second_flat = second_q.reshape(half_rows * GROUP, HD)
    first_qpos = jnp.repeat(first_pos, GROUP)
    second_qpos = jnp.repeat(second_pos, GROUP)
    flat_rows = half_rows * GROUP
    empty = (
        jnp.full((flat_rows,), -1e30, jnp.float32),
        jnp.zeros((flat_rows,), jnp.float32),
        jnp.zeros((flat_rows, HD), jnp.float32),
    )
    carried = (empty, empty)
    offset = jnp.int32(0)
    keys_in = lax.all_gather(key_part, "ctx", axis=0, tiled=True)
    values_in = lax.all_gather(value_part, "ctx", axis=0, tiled=True)
    updated = []
    for softmax_state, query_flat, query_pos in (
        (carried[0], first_flat, first_qpos),
        (carried[1], second_flat, second_qpos),
    ):
        step_fn = partial(
            update_state,
            query_flat=query_flat,
            query_pos=query_pos,
            keys_in=keys_in,
            values_in=values_in,
            offset=offset,
        )
        updated.append(lax.cond(offset <= jnp.max(query_pos), step_fn, keep_state, softmax_state))

    def finish(softmax_state):
        return (
            (softmax_state[2] / softmax_state[1][:, None])
            .astype(jnp.bfloat16)
            .reshape(half_rows, GROUP * HD)
        )

    first_out = finish(updated[0])
    second_out = finish(updated[1])
    attended = jnp.concatenate([first_out, second_out], axis=0)
    partial_model = jnp.dot(
        attended,
        lax.all_gather(weight_out, "ctx", axis=1, tiled=True),
        preferred_element_type=jnp.float32,
    )
    positions = ctx_id * tok_rows + jnp.arange(tok_rows, dtype=jnp.int32)[:, None]
    starts = join[None, :]
    inside = (positions >= starts) & (positions < starts + FRAME)
    frame_base = (jnp.arange(join.shape[0], dtype=jnp.int32) * FRAME)[None, :]
    source = jnp.sum(jnp.where(inside, frame_base + positions - starts, 0), axis=1)
    is_vision = jnp.any(inside, axis=1)

    def vision_term():
        frame_in = frames.astype(jnp.float32)
        center = jnp.mean(frame_in, axis=1, keepdims=True)
        spread = jnp.mean((frame_in - center) * (frame_in - center), axis=1, keepdims=True)
        normed_frames = ((frame_in - center) * lax.rsqrt(spread + 1e-06) * ln_gain).astype(
            jnp.bfloat16
        )
        vis_width = w_proj.shape[0]
        normed_half = lax.dynamic_slice_in_dim(normed_frames, tp_id * vis_width, vis_width, 1)
        projected = jnp.dot(normed_half, w_proj, preferred_element_type=jnp.float32)
        return jnp.where(is_vision[:, None], jnp.take(projected, source, axis=0), 0.0)

    def model_term():
        return partial_model

    is_first = segment_id == 0
    section_term = lax.cond(is_first, vision_term, model_term)
    baseline = jnp.where(
        is_first, jnp.where(is_vision[:, None], b_proj[None, :], text.astype(jnp.float32)), inputs
    )
    summed = lax.psum(section_term.astype(jnp.bfloat16), "tp").astype(jnp.float32)
    result = (baseline + summed).astype(jnp.bfloat16)
    return result[None]


def relay_kernel(
    sizes,
    held, text, frames, join, ln_gain, w_proj, b_proj, norm_gain, w_qkv, b_qkv, w_out,
    out,
    held_v, rs_out, rs_in, x_v, wq_v, wo_v, own_part, part_out, part_in, q_v, kv_v, att_v,
    vis_v, wp_v, text_v, half_out, half_in, half_own, res_out, res_v, both, vis_out, vis_in, vis_own,
    load_sem, store_sem, x_send, x_recv, rs_send, rs_recv, fwd_send, fwd_recv,
    part_send, part_recv, kv_send, kv_recv, att_send, att_recv,
    half_send, half_recv, res_send, res_recv, pair_send, pair_recv, vis_send, vis_recv,
):
    segs, n, rows, width = sizes
    unit = rows // 2
    half = unit // 2
    last = segs - 1
    s = lax.axis_index("segment")
    c = lax.axis_index("ctx")
    t = lax.axis_index("tp")
    owner = jnp.where(s == 0, last, s)
    layer = owner - 1
    runs = (s < last, s > 0)
    feeds = s < last
    query_cols = GROUP * HD

    def remote(src, dst, send, recv, segment, ctx, tp):
        return pltpu.make_async_remote_copy(
            src_ref=src, dst_ref=dst, send_sem=send, recv_sem=recv,
            device_id={"segment": segment, "ctx": ctx, "tp": tp},
            device_id_type=pl.DeviceIdType.MESH,
        )

    def cols(k):
        return pl.ds(pl.multiple_of(k * width, 128), width)

    def strip(r, side):
        return pl.ds(pl.multiple_of(r * unit + side * half, 16), half)

    def turn(d):
        return lax.rem(c + d, n)

    def far_first(i):
        return jnp.where(2 * c < n, n - 1 - i, i)

    def near_first(i):
        return jnp.where(2 * c < n, i, n - 1 - i)

    loads = {
        "held": pltpu.make_async_copy(held, held_v, load_sem.at[0]),
        "wq": pltpu.make_async_copy(w_qkv.at[layer], wq_v, load_sem.at[1]),
        "wo": pltpu.make_async_copy(w_out.at[layer], wo_v, load_sem.at[2]),
        "wp": pltpu.make_async_copy(w_proj, wp_v, load_sem.at[3]),
        "text": pltpu.make_async_copy(text, text_v, load_sem.at[4]),
    }
    barrier = pltpu.get_barrier_semaphore()

    def greet(segment, ctx, tp):
        pl.semaphore_signal(
            barrier, inc=1, device_id={"segment": segment, "ctx": ctx, "tp": tp},
            device_id_type=pl.DeviceIdType.MESH,
        )

    greet(s, c, 1 - t)
    for d in range(1, n):
        greet(s, turn(d), t)
    for e in range(1, segs):
        for d in range(n):
            greet(lax.rem(s + e, segs), turn(d), t)

    @pl.when(feeds)
    def _():
        loads["held"].start()

    loads["wq"].start()
    loads["wo"].start()

    @pl.when(s == 0)
    def _():
        loads["wp"].start()
        loads["text"].start()

    for k in range(n):
        @pl.when(k > c)
        def _():
            kv_v[k] = jnp.zeros((2, unit, 2 * HD), jnp.bfloat16)

    kv_v[c, 1] = jnp.zeros((unit, 2 * HD), jnp.bfloat16)

    pl.semaphore_wait(barrier, segs * n)

    def x_copy(r, k):
        worker = jnp.where(s == last - 1, 0, s + 1) if r == 0 else jnp.minimum(s + 1, last)
        return remote(
            held.at[strip(r, t), cols(k)], x_v.at[c, r, t],
            x_send.at[r, k], x_recv.at[r, c], worker, k, t,
        )

    def rs_copy(to, slot):
        return remote(rs_out, rs_in, rs_send.at[slot], rs_recv.at[0], to, c, t)

    def fwd_copy(r, j, side):
        return remote(
            x_v.at[j, r, side], x_v.at[j, r, side], fwd_send.at[r, j], fwd_recv.at[r, j],
            s, c, 1 - t,
        )

    def part_copy(r, k, to, slot):
        return remote(
            part_out.at[r, k], part_in.at[r, slot], part_send.at[r, k], part_recv.at[r, slot],
            s, to, t,
        )

    def part_wait(r, slot):
        part_copy(r, c, turn(1), slot).wait_recv()

    def send_part(r, k):
        @pl.when(k > c)
        def _():
            part_copy(r, k, jnp.minimum(c + 1, n - 1), k).start()

        @pl.when(k < c)
        def _():
            to = jnp.maximum(c - 1, 0)
            part_copy(r, k, to, jnp.where(k == to, n, k)).start()

    def kv_copy(r, to, k, slot, side):
        return remote(
            kv_v.at[slot, r], kv_v.at[slot, r], kv_send.at[r, side, k], kv_recv.at[r, slot],
            to, k, t,
        )

    def att_copy(r, to, slot, sem):
        return remote(
            att_v.at[slot, r], att_v.at[slot, r], att_send.at[r, sem], att_recv.at[r, slot],
            s, to, t,
        )

    up, down = jnp.minimum(c + 1, n - 1), jnp.maximum(c - 1, 0)

    def each_hop(r, j, act):
        @pl.when((j <= c) & (c < n - 1))
        def _():
            act(att_copy(r, up, j, j))

        @pl.when((j == c) & (c > 0))
        def _():
            act(att_copy(r, down, j, n))

        @pl.when((j > c) & (c > 0))
        def _():
            act(att_copy(r, down, j, j))

    def half_copy(r, j):
        return remote(
            half_out.at[r, j], half_in.at[r, j], half_send.at[r, j], half_recv.at[r, j],
            s, c, 1 - t,
        )

    def vis_copy(k):
        return remote(vis_out.at[k], vis_in.at[k], vis_send.at[k], vis_recv.at[k], s, c, 1 - t)

    def res_copy(r, j, slot):
        return remote(
            res_out.at[r, j], res_v.at[slot, r, t], res_send.at[r, j], res_recv.at[r, slot],
            owner, j, t,
        )

    def pair_copy(r, k, side):
        return remote(
            res_v.at[k, r, side], res_v.at[k, r, side], pair_send.at[r, k], pair_recv.at[r, k],
            s, c, 1 - t,
        )

    def out_copy(r, k, side):
        return pltpu.make_async_copy(
            res_v.at[k, r, side], out.at[strip(r, side), cols(k)], store_sem.at[r, k, side]
        )

    @pl.when(feeds)
    def _():
        for r in range(2):
            for d in range(n):
                x_copy(r, turn(d)).start()
        loads["held"].wait()

        @pl.loop(0, rows // 32)
        def _(i):
            at = pl.ds(pl.multiple_of(i * 32, 32), 32)
            x = held_v[at, :].astype(jnp.float32)
            scale = lax.rsqrt(jnp.mean(x * x, axis=1, keepdims=True) + 1e-06)
            rs_out[at, :] = jnp.broadcast_to(scale, (32, HD))

        rs_copy(s + 1, 0).start()

        @pl.when(s == last - 1)
        def _():
            rs_copy(0, 1).start()

    loads["wq"].wait()
    gain = norm_gain[pl.ds(layer, 1), cols(c)]
    bias = b_qkv[pl.ds(layer, 1), :]

    def hand_over(r, i):
        @pl.when(runs[r])
        def _():
            j = turn(i)
            remote(
                x_v.at[j, r, t], x_v.at[j, r, t], x_send.at[r, j], x_recv.at[r, j], s, c, 1 - t
            ).wait_recv()
            fwd_copy(r, j, t).start()

    def multiply(r, i):
        @pl.when(runs[r])
        def _():
            j = far_first(i)
            fwd_copy(r, j, 1 - t).wait_recv()
            x = x_v[j, r].reshape(unit, width).astype(jnp.float32)
            product = jnp.dot(
                (x * gain).astype(jnp.bfloat16), wq_v[...], preferred_element_type=jnp.float32
            )
            own_part[r, j] = product

            @pl.when(((c == 0) | (c == n - 1)) & (j != c))
            def _():
                part_out[r, j] = product.astype(jnp.bfloat16)
                send_part(r, j)

    def pass_part(r, i):
        j = far_first(i)

        @pl.when(runs[r] & (c > 0) & (c < n - 1) & (j != c))
        def _():
            part_wait(r, j)
            part_out[r, j] = (
                own_part[r, j] + part_in[r, j].astype(jnp.float32)
            ).astype(jnp.bfloat16)
            send_part(r, j)

    @pl.loop(0, n)
    def _(i):
        hand_over(0, i)

    @pl.loop(0, n)
    def _(i):
        multiply(0, i)
        hand_over(1, i)

    @pl.when(s == 0)
    def _():
        frame_in = frames[...].astype(jnp.float32)
        center = jnp.mean(frame_in, axis=1, keepdims=True)
        spread = jnp.mean((frame_in - center) * (frame_in - center), axis=1, keepdims=True)
        normed = ((frame_in - center) * lax.rsqrt(spread + 1e-06) * ln_gain[...]).astype(
            jnp.bfloat16
        )
        vis_width = w_proj.shape[0]
        normed = jnp.where(t == 0, normed[:, :vis_width], normed[:, vis_width:])
        count = frames.shape[0]
        token = lax.broadcasted_iota(jnp.int32, (unit, count), 1)
        row = lax.broadcasted_iota(jnp.int32, (unit, count), 0)
        row = jnp.where(row < half, row, row + half)
        for side in range(2):
            position = c * rows + side * half + row
            pick = jnp.zeros((unit, count), jnp.float32)
            for f in range(count // FRAME):
                mine = (token >= f * FRAME) & (token < (f + 1) * FRAME)
                hit = mine & (position - join[f] == token - f * FRAME)
                pick = jnp.where(hit, 1.0, pick)
            vis_v[side] = jnp.dot(
                pick.astype(jnp.bfloat16), normed, preferred_element_type=jnp.float32
            ).astype(jnp.bfloat16)
        loads["wp"].wait()
        loads["text"].wait()

        @pl.loop(0, n)
        def _(k):
            vis_out[k] = jnp.dot(
                vis_v[1 - t], wp_v[:, cols(k)], preferred_element_type=jnp.float32
            ).astype(jnp.bfloat16)
            vis_copy(k).start()
            vis_own[k] = jnp.dot(vis_v[t], wp_v[:, cols(k)], preferred_element_type=jnp.float32)

    @pl.loop(0, n)
    def _(i):
        multiply(1, i)
        pass_part(0, i)

    def merge(r):
        @pl.when(runs[r])
        def _():
            @pl.when(c > 0)
            def _():
                part_wait(r, c)
                own_part[r, c] += part_in[r, c].astype(jnp.float32)

            @pl.when(c < n - 1)
            def _():
                part_wait(r, n)
                own_part[r, c] += part_in[r, n].astype(jnp.float32)

            scale = rs_in[r * unit : (r + 1) * unit, :1]
            merged = (own_part[r, c] * scale + bias).astype(jnp.bfloat16)
            q_v[r] = merged[:, :query_cols]
            kv_v[c, r] = merged[:, query_cols:]
            for k in range(n):
                @pl.when(k > c)
                def _():
                    kv_copy(r, s, k, c, 0).start()

                @pl.when((k > c) & (owner == last))
                def _():
                    kv_copy(r, last - s, k, c, 1).start()

            if r == 0:
                @pl.when(s == 0)
                def _():
                    kv_copy(0, last, c, c, 1).start()

    def attend(r):
        @pl.when(runs[r])
        def _():
            take = (s < last) if r == 0 else (s == last)
            for k in range(n):
                @pl.when((k < c) & take)
                def _():
                    for part in range(2):
                        kv_copy(part, s, turn(1), k, 0).wait_recv()

            if r == 1:
                @pl.when(s == last)
                def _():
                    kv_copy(0, s, turn(1), c, 0).wait_recv()

            first = c * rows + r * unit
            query_pos = first + lax.broadcasted_iota(jnp.int32, (unit, n * rows), 0)
            allowed = lax.broadcasted_iota(jnp.int32, (unit, n * rows), 1) <= query_pos
            keys = kv_v[:, :, :, :HD].reshape(n * rows, HD)
            values = kv_v[:, :, :, HD:].reshape(n * rows, HD)
            for h in range(GROUP):
                q = q_v[r, :, h * HD : (h + 1) * HD]
                scores = lax.dot_general(
                    q, keys, (((1,), (1,)), ((), ())), preferred_element_type=jnp.float32
                ) * HD ** (-0.5)
                scores = jnp.where(allowed, scores, -1e30)
                weights = jnp.exp(scores - jnp.max(scores, axis=1, keepdims=True))
                total = jnp.sum(weights, axis=1, keepdims=True)
                mixed = jnp.dot(
                    weights.astype(jnp.bfloat16), values, preferred_element_type=jnp.float32
                ) / total
                att_v[c, r, :, h * HD : (h + 1) * HD] = mixed.astype(jnp.bfloat16)
            each_hop(r, c, lambda copy: copy.start())

    remote(rs_out, rs_in, rs_send.at[0], rs_recv.at[0], s, c, 1 - t).wait_recv()
    merge(0)

    @pl.loop(0, n)
    def _(i):
        pass_part(1, i)

    merge(1)
    attend(0)
    attend(1)

    @pl.when(s == 0)
    def _():
        row = lax.broadcasted_iota(jnp.int32, (half, width), 0)

        @pl.loop(0, n)
        def _(k):
            vis_copy(k).wait_recv()
            total = vis_own[k] + vis_in[k].astype(jnp.float32) + b_proj[cols(k)][None]
            for r in range(2):
                place = c * rows + r * unit + t * half + row
                inside = jnp.zeros((half, width), jnp.bool_)
                for f in range(frames.shape[0] // FRAME):
                    inside = inside | ((place >= join[f]) & (place < join[f] + FRAME))
                base = text_v[strip(r, t), cols(k)].astype(jnp.float32)
                res_v[k, r, t] = jnp.where(
                    inside, total[r * half : (r + 1) * half], base
                ).astype(jnp.bfloat16)
                pair_copy(r, k, t).start()
                out_copy(r, k, t).start()

    def project(r, i):
        @pl.when(runs[r])
        def _():
            j = near_first(i)

            @pl.when(j != c)
            def _():
                att_copy(r, turn(1), j, j).wait_recv()
                each_hop(r, j, lambda copy: copy.start())

            both[...] = jnp.dot(
                att_v[j, r], wo_v[...], preferred_element_type=jnp.float32
            ).reshape(2, half, width)
            half_out[r, j] = both[1 - t].astype(jnp.bfloat16)
            half_copy(r, j).start()
            half_own[r, j] = x_v[j, r, t].astype(jnp.float32) + both[t]

    def deliver(r, i):
        @pl.when(runs[r])
        def _():
            j = near_first(i)
            half_copy(r, j).wait_recv()
            total = (half_own[r, j] + half_in[r, j].astype(jnp.float32)).astype(jnp.bfloat16)

            @pl.when((j == c) & (s > 0))
            def _():
                res_v[c, r, t] = total
                pair_copy(r, c, t).start()
                out_copy(r, c, t).start()

            @pl.when((j != c) | (s == 0))
            def _():
                res_out[r, j] = total
                res_copy(r, j, c).start()

    def collect(r, i):
        k = near_first(i)

        @pl.when((s > 0) & ((k != c) | ((s == last) & (r == 0))))
        def _():
            remote(
                res_out.at[r, k], res_v.at[k, r, t], res_send.at[r, k], res_recv.at[r, k],
                s, c, 1 - t,
            ).wait_recv()
            pair_copy(r, k, t).start()
            out_copy(r, k, t).start()

    loads["wo"].wait()

    @pl.loop(0, n)
    def _(i):
        project(0, i)

    @pl.loop(0, n)
    def _(i):
        deliver(0, i)
        project(1, i)

    @pl.loop(0, n)
    def _(i):
        deliver(1, i)
        collect(0, i)

    @pl.loop(0, n)
    def _(i):
        collect(1, i)

    for r in range(2):
        @pl.loop(0, n)
        def _(d):
            k = turn(d)
            pair_copy(r, k, 1 - t).wait_recv()
            out_copy(r, k, 1 - t).start()

    @pl.when(feeds)
    def _():
        for r in range(2):
            for k in range(n):
                x_copy(r, k).wait_send()
        rs_copy(s + 1, 0).wait_send()

        @pl.when(s == last - 1)
        def _():
            rs_copy(0, 1).wait_send()

    @pl.when(s == 0)
    def _():
        kv_copy(0, last, c, c, 1).wait_send()
        for k in range(n):
            vis_copy(k).wait_send()

    for r in range(2):
        @pl.when(runs[r])
        def _():
            @pl.loop(0, n)
            def _(d):
                j = turn(d)
                fwd_copy(r, j, t).wait_send()
                half_copy(r, j).wait_send()

                @pl.when(d > 0)
                def _():
                    part_copy(r, j, turn(1), c).wait_send()

                each_hop(r, j, lambda copy: copy.wait_send())

                @pl.when((d > 0) | (s == 0))
                def _():
                    res_copy(r, j, c).wait_send()

                @pl.when(j > c)
                def _():
                    kv_copy(r, s, j, c, 0).wait_send()

                @pl.when((j > c) & (owner == last))
                def _():
                    kv_copy(r, last - s, j, c, 1).wait_send()

        @pl.loop(0, n)
        def _(k):
            pair_copy(r, k, t).wait_send()
            out_copy(r, k, 0).wait()
            out_copy(r, k, 1).wait()


def relayed(sizes, held, text, frames, join, ln_gain, w_proj, b_proj, norm_gain, w_qkv, b_qkv, w_out):
    segs, n, rows, width = sizes
    unit = rows // 2
    half = unit // 2
    depth, qkv = w_qkv.shape[1:]
    bf16, f32 = jnp.bfloat16, jnp.float32
    hbm = pl.BlockSpec(memory_space=pl.ANY)
    vmem = pl.BlockSpec(memory_space=pltpu.VMEM)
    smem = pl.BlockSpec(memory_space=pltpu.SMEM)
    dma = pltpu.SemaphoreType.DMA
    out = pl.pallas_call(
        partial(relay_kernel, sizes),
        out_shape=jax.ShapeDtypeStruct((rows, n * width), bf16),
        in_specs=[hbm, hbm, vmem, smem, vmem, hbm, vmem, vmem, hbm, vmem, hbm],
        out_specs=hbm,
        scratch_shapes=[
            pltpu.VMEM((rows, n * width), bf16),
            pltpu.VMEM((rows, HD), f32),
            pltpu.VMEM((rows, HD), f32),
            pltpu.VMEM((n, 2, 2, half, width), bf16),
            pltpu.VMEM((depth, qkv), bf16),
            pltpu.VMEM(w_out.shape[1:], bf16),
            pltpu.VMEM((2, n, unit, qkv), f32),
            pltpu.VMEM((2, n, unit, qkv), bf16),
            pltpu.VMEM((2, n + 1, unit, qkv), bf16),
            pltpu.VMEM((2, unit, GROUP * HD), bf16),
            pltpu.VMEM((n, 2, unit, 2 * HD), bf16),
            pltpu.VMEM((n, 2, unit, GROUP * HD), bf16),
            pltpu.VMEM((2, unit, w_proj.shape[0]), bf16),
            pltpu.VMEM(w_proj.shape, bf16),
            pltpu.VMEM((rows, n * width), bf16),
            pltpu.VMEM((2, n, half, width), bf16),
            pltpu.VMEM((2, n, half, width), bf16),
            pltpu.VMEM((2, n, half, width), f32),
            pltpu.VMEM((2, n, half, width), bf16),
            pltpu.VMEM((n, 2, 2, half, width), bf16),
            pltpu.VMEM((2, half, width), f32),
            pltpu.VMEM((n, unit, width), bf16),
            pltpu.VMEM((n, unit, width), bf16),
            pltpu.VMEM((n, unit, width), f32),
            dma((5,)), dma((2, n, 2)), dma((2, n)), dma((2, n)), dma((2,)), dma((1,)),
            dma((2, n)), dma((2, n)), dma((2, n)), dma((2, n + 1)), dma((2, 2, n)), dma((2, n)),
            dma((2, n + 1)), dma((2, n)), dma((2, n)), dma((2, n)), dma((2, n)), dma((2, n)),
            dma((2, n)), dma((2, n)), dma((n,)), dma((n,)),
        ],
        compiler_params=pltpu.CompilerParams(
            collective_id=0, has_side_effects=True, vmem_limit_bytes=60 * 1024 * 1024
        ),
    )(
        held[0], text, frames, join, ln_gain[None], w_proj, b_proj, norm_gain, w_qkv, b_qkv, w_out
    )
    return out[None]


def section(held, text, frames, join, ln_gain, w_proj, b_proj, norm_gain, w_qkv, b_qkv, w_out):
    segs, n = lax.axis_size("segment"), lax.axis_size("ctx")
    rows, width = held.shape[1], held.shape[2] // n
    args = (held, text, frames, join, ln_gain, w_proj, b_proj, norm_gain, w_qkv, b_qkv, w_out)
    whole_tiles = width % 128 == 0 and rows % 64 == 0 and w_proj.shape[0] % 128 == 0
    if whole_tiles and n * rows <= 1024 and lax.axis_size("tp") == 2 and segs > 2:
        return relayed((segs, n, rows, width), *args)
    return on_device(*args)


def solution(mesh):
    return jax.shard_map(
        section,
        mesh=mesh,
        in_specs=(
            P("segment", "ctx", None),
            P("ctx", None),
            P("ctx", None),
            P("ctx"),
            P(),
            P("tp", None),
            P(),
            P(),
            P(None, "ctx", "tp"),
            P(None, "tp"),
            P(None, "tp", "ctx"),
        ),
        out_specs=P("segment", "ctx", None),
        check_vma=False,
    )
```
